128 devices in a mesh: dp: 8 (over x, core), fsdp: 16 (over y, z).
Axes of the slice: x: 4, y: 4, z: 4, core: 2. Of those that a mesh axis runs over, the one named last changes fastest.
Arguments:
- grads: bfloat16 [8, 2, 8192, 1024], P('dp', None, 'fsdp')
- error: bfloat16 [8, 2, 8192, 1024], P('dp', None, 'fsdp'), may hold values from -4 to 4
- proj_old: float32 [2, 8192, 256], P(None, 'fsdp'), may hold values from -0.0625 to 0.0625
- moment1: float32 [2, 256, 1024], replicated, may hold values from -4 to 4
- moment2: float32 [2, 256, 1024], replicated, may hold values from 0.1 to 10
Outputs:
- update: bfloat16 [2, 8192, 1024], P(None, 'fsdp')
- error_new: bfloat16 [8, 2, 8192, 1024], P('dp', None, 'fsdp')
- proj_new: float32 [2, 8192, 256], P(None, 'fsdp')
- moment1_new: float32 [2, 256, 1024], replicated
- moment2_new: float32 [2, 256, 1024], replicated
The draws below stay inside these ranges and needn't reach their ends.
All inputs are finite; a program needn't handle non-finite values.
Results may differ from the reference program's by a relative error of at most 0.0014.
Values sent between devices are 32-bit elements; how exact they have to be, the bound alone decides.
A program may use at most 128 MiB of HBM per device.

```python
import math
import jax
import jax.numpy as jnp
from jax import lax

N = 1024
R = 256
MATS = 2
ITERS = 2
ROWS = 8192
REPLICAS = 8


def draw_grads(key, part):
    key = jax.random.fold_in(key, 7)
    first, second = jax.random.split(key)
    shape = (REPLICAS, MATS, ROWS, N)
    base = jax.random.normal(first, shape, jnp.float32)
    scales = jnp.exp(jax.random.uniform(second, (REPLICAS, MATS, ROWS, 1), jnp.float32, 0.0, math.log(10.0)))
    rising = 1.0 + 2.0 * jnp.arange(ROWS, dtype=jnp.float32).reshape(1, 1, ROWS, 1) / (ROWS - 1)
    return (0.3 * base * scales * rising).astype(jnp.bfloat16)


def steps_of(stream_key, dims, shards, least, largest):
    loudness, own = 1.0, jax.random.fold_in(stream_key, 6)
    for axis_at, blocks in shards:
        heights = jnp.exp(jax.random.uniform(jax.random.fold_in(own, axis_at), (blocks,), jnp.float32, least / len(shards), largest / len(shards)))
        loudness = loudness * jnp.repeat(heights, dims[axis_at] // blocks).reshape([-1 if axis == axis_at else 1 for axis in range(len(dims))])
    return loudness


def normal_values(own_key, extent, deviation, reach, cuts=(), held_as=jnp.bfloat16):
    entries = deviation * jax.random.normal(own_key, extent, jnp.float32)
    if cuts:
        entries = entries * steps_of(own_key, extent, cuts, -0.22, 0.18)
    return jnp.clip(entries, -reach, reach).astype(held_as)


def setup_inputs(seed: int = 0) -> dict:
    keys = jax.random.split(jax.random.key(seed), 6)
    grads = draw_grads(jax.random.fold_in(keys[5], 71), 0)
    error = normal_values(keys[1], (REPLICAS, MATS, ROWS, N), 0.3, 4.0, ((0, 8), (2, 16)))
    proj_old = normal_values(keys[2], (MATS, ROWS, R), ROWS ** -0.5, 0.0625, ((1, 16),), jnp.float32)
    moment1 = normal_values(keys[3], (MATS, R, N), 0.3, 4.0, (), jnp.float32)
    moment2 = jnp.clip(jnp.exp(jax.random.uniform(keys[4], (MATS, R, N), jnp.float32, math.log(0.1), math.log(10.0))), 0.1, 10.0)
    return {"grads": grads, "error": error, "proj_old": proj_old, "moment1": moment1, "moment2": moment2}


precise = lax.Precision.HIGHEST

def tri_left(factor, right):
    return lax.linalg.triangular_solve(factor, right, left_side=True, lower=True)

def adam_moments(rotation, moment1, moment2, grad_proj):
    turned = jnp.einsum('krs,ksn->krn', rotation, moment1, precision=precise)
    spread = jnp.abs(moment2 - moment1 * moment1)
    second = jnp.einsum('krs,ksn->krn', rotation * rotation, spread, precision=precise) + turned * turned
    first_new = 0.9 * turned + 0.1 * grad_proj
    second_new = 0.99 * second + 0.01 * grad_proj * grad_proj
    return (first_new, second_new, first_new / (jnp.sqrt(second_new) + 1e-06))

def reference(grads, error, proj_old, moment1, moment2):
    accrued = grads.astype(jnp.float32) + error.astype(jnp.float32)
    current = proj_old
    for step in range(ITERS):
        columns = jnp.einsum('pkmn,kmr->knr', accrued, current, precision=precise)
        widened = jnp.einsum('pkmn,knr->kmr', accrued, columns, precision=precise)
        gram = jnp.einsum('kmr,kms->krs', widened, widened, precision=precise)
        factor = jnp.linalg.cholesky(gram)
        current = jnp.swapaxes(tri_left(factor, jnp.swapaxes(widened, 1, 2)), 1, 2)
    rotation = jnp.einsum('kmr,kms->krs', current, proj_old, precision=precise)
    local_proj = jnp.einsum('kmr,pkmn->pkrn', current, accrued, precision=precise)
    back = jnp.einsum('kmr,pkrn->pkmn', current, local_proj, precision=precise)
    error_new = (accrued - back).astype(jnp.bfloat16)
    grad_proj = lax.optimization_barrier(jnp.sum(local_proj, axis=0)) / REPLICAS
    first_new, second_new, stepped = adam_moments(rotation, moment1, moment2, grad_proj)
    update = jnp.einsum('kmr,krn->kmn', current, stepped, precision=precise).astype(jnp.bfloat16)
    return (update, error_new, current, first_new, second_new)
```

```python
import functools
import jax
import jax.numpy as jnp
from jax import lax
from jax.experimental import pallas as pl
from jax.experimental.pallas import tpu as pltpu
from jax.sharding import PartitionSpec as P

F32 = jnp.float32
BF16 = jnp.bfloat16
MESH = pl.DeviceIdType.MESH
N = 1024
R = 256
ROWS = 512
PIECE = 128
BLOCK = 64
COPIES = 176


def dot(a, b, ca=1, cb=0):
    return lax.dot_general(
        a,
        b,
        (((ca,), (cb,)), ((), ())),
        precision=lax.Precision.HIGHEST,
        preferred_element_type=F32,
    )


def halves(value):
    high = value.astype(BF16)
    return high, (value - high.astype(F32)).astype(BF16)


def dot_bf16(a, b, ca=1, cb=0):
    return lax.dot_general(a, b, (((ca,), (cb,)), ((), ())), preferred_element_type=F32)


def dot3(a, b, ca=1, cb=0):
    ah, al = halves(a)
    bh, bl = halves(b)
    small = dot_bf16(ah, bl, ca, cb) + dot_bf16(al, bh, ca, cb)
    return dot_bf16(ah, bh, ca, cb) + small


class Place:
    def __init__(self):
        dp, fsdp = lax.axis_index("dp"), lax.axis_index("fsdp")
        self.at = {
            "x": lax.div(dp, 2),
            "c": lax.rem(dp, 2),
            "y": lax.div(fsdp, 4),
            "z": lax.rem(fsdp, 4),
        }

    def peer(self, axis, step):
        new = dict(self.at)
        c = self.at["c"]
        if axis == "c":
            new["c"] = 1 - c
        elif axis == "a":
            new["z"] = lax.rem(new["z"] + (1 - c) * step, 4)
            new["y"] = lax.rem(new["y"] + c * step, 4)
        elif axis == "b":
            new["z"] = lax.rem(new["z"] + c * step, 4)
            new["y"] = lax.rem(new["y"] + (1 - c) * step, 4)
        else:
            new[axis] = lax.rem(new[axis] + step, 4)
        return (new["x"] * 2 + new["c"], new["y"] * 4 + new["z"])

    def index(self, axis):
        c, y, z = self.at["c"], self.at["y"], self.at["z"]
        if axis == "a":
            return z * (1 - c) + y * c
        if axis == "b":
            return y * (1 - c) + z * c
        return self.at[axis]


class Links:
    def __init__(self, place, send_sems, recv_sems):
        self.place, self.send_sems, self.recv_sems = place, send_sems, recv_sems
        self.used = 0
        self.started = []

    def send(self, src, dst, axis, step):
        at = self.used
        self.used += 1
        copy = pltpu.make_async_remote_copy(
            src_ref=src,
            dst_ref=dst,
            send_sem=self.send_sems.at[at],
            recv_sem=self.recv_sems.at[at],
            device_id=self.place.peer(axis, step),
            device_id_type=MESH,
        )
        copy.start()
        self.started.append(copy)
        return copy

    def drain(self):
        assert self.used <= COPIES
        for copy in self.started:
            copy.wait_send()


def rows_of(index, size):
    return pl.ds(pl.multiple_of(index * size, size), size)


class Reduce:
    def __init__(self, links, src, out, lanes, axes, scratch):
        self.links, self.src, self.out, self.lanes, self.axes = links, src, out, lanes, axes
        self.first, self.mine, self.second, self.last = scratch
        self.copies = None

    def start(self):
        axis = self.axes[0]
        me = self.links.place.index(axis)
        self.copies = []
        for step in (2, 1, 3):
            block = rows_of(lax.rem(me + step, 4), 64)
            self.copies.append(
                self.links.send(self.src.at[block, self.lanes], self.first.at[step - 1], axis, step)
            )

    def wait(self):
        for copy in self.copies:
            copy.wait_recv()

    def second_stage(self):
        self.wait()
        place = self.links.place
        me = place.index(self.axes[0])
        total = self.src[rows_of(me, 64), self.lanes]
        for slot in range(3):
            total = total + self.first[slot]
        self.mine[...] = total
        axis = self.axes[1]
        me = place.index(axis)
        self.copies = []
        for step in (2, 1, 3):
            block = rows_of(lax.rem(me + step, 4), 16)
            self.copies.append(
                self.links.send(self.mine.at[block], self.second.at[step - 1], axis, step)
            )

    def own_rows(self):
        place = self.links.place
        start = place.index(self.axes[0]) * 64 + place.index(self.axes[1]) * 16
        return pl.ds(pl.multiple_of(start, 16), 16)

    def third_stage(self):
        self.wait()
        place = self.links.place
        me = place.index(self.axes[1])
        total = self.mine[rows_of(me, 16)]
        for slot in range(3):
            total = total + self.second[slot]
        if len(self.axes) == 2:
            self.out[self.own_rows(), self.lanes] = total
            return
        axis = self.axes[2]
        me = place.index(axis)
        self.last[me] = total
        self.copies = []
        for step in (2, 1, 3):
            self.copies.append(self.links.send(self.last.at[me], self.last.at[me], axis, step))

    def gather_second(self):
        if len(self.axes) == 3:
            self.wait()
            self.out[self.own_rows(), self.lanes] = (
                (self.last[0] + self.last[1]) + (self.last[2] + self.last[3])
            )
        own = self.out.at[self.own_rows(), self.lanes]
        self.copies = [self.links.send(own, own, self.axes[1], step) for step in (2, 1, 3)]

    def gather_first(self):
        self.wait()
        axis = self.axes[0]
        own = self.out.at[rows_of(self.links.place.index(axis), 64), self.lanes]
        self.copies = [self.links.send(own, own, axis, step) for step in (2, 1, 3)]


def stages(parts):
    for part in parts:
        part.start()
    yield
    for part in parts:
        part.second_stage()
    yield
    for part in parts:
        part.third_stage()
    yield
    for part in parts:
        part.gather_second()
    yield
    for part in parts:
        part.gather_first()
    yield
    for part in parts:
        part.wait()
    yield


def run_all(steps):
    for _ in steps:
        pass


def eliminate(diag):
    rows = lax.broadcasted_iota(jnp.int32, (BLOCK, 2 * BLOCK), 0)
    lanes = lax.broadcasted_iota(jnp.int32, (BLOCK, 2 * BLOCK), 1)
    identity = (lanes == rows + BLOCK).astype(F32)
    state = jnp.concatenate([diag, identity[:, BLOCK:]], axis=1)
    pivots = jnp.ones((BLOCK, 2 * BLOCK), F32)
    for at in range(BLOCK):
        column = jnp.broadcast_to(state[:, at : at + 1], (BLOCK, 2 * BLOCK))
        pivot = jnp.broadcast_to(column[at : at + 1, :], (BLOCK, 2 * BLOCK))
        row = jnp.broadcast_to(state[at : at + 1, :], (BLOCK, 2 * BLOCK))
        pivots = jnp.where(rows == at, pivot, pivots)
        factor = jnp.where(rows > at, column * (1.0 / pivot), 0.0)
        state = state - factor * row
    return (state * lax.rsqrt(pivots))[:, BLOCK:]


def inverse_factor(work):
    rows = lax.broadcasted_iota(jnp.int32, (R, R), 0)
    lanes = lax.broadcasted_iota(jnp.int32, (R, R), 1)
    work[:, R:] = (rows == lanes).astype(F32)
    for block in range(R // BLOCK):
        low, high = block * BLOCK, (block + 1) * BLOCK
        scale = eliminate(work[low:high, low:high])
        strip = dot(scale, work[low:high, :])
        work[low:high, :] = strip
        if high < R:
            work[high:, :] = work[high:, :] - dot(strip[:, high:R], strip, 0, 0)


def main_kernel(
    grads, error, proj_old, wide, local, summed, mixer, cross, a_send, a_recv, pair, s_recv, total,
    bufs, outs, normal, work, gram, unmixed, first, mine, second, last, ufirst, umine, usecond,
    ubuf, send_sems, recv_sems,
):
    place = Place()
    links = Links(place, send_sems, recv_sems)
    c, x = place.at["c"], place.at["x"]
    other = 1 - c

    barrier = pltpu.get_barrier_semaphore()
    partners = [("c", 1)] + [(axis, step) for axis in "xyz" for step in (1, 2, 3)]
    for axis, step in partners:
        pl.semaphore_signal(barrier, inc=1, device_id=place.peer(axis, step), device_id_type=MESH)

    order = (2, 1, 3, 0)
    blocks = [rows_of(lax.rem(x + step, 4), PIECE) for step in order]
    for rows in blocks:
        a_send[rows, :] = grads[other, rows, :].astype(F32) + error[other, rows, :].astype(F32)
    pl.semaphore_wait(barrier, len(partners))
    core_copies = [links.send(a_send.at[rows], a_recv.at[rows], "c", 1) for rows in blocks]
    s_copies = []
    for step, rows, copy in zip(order, blocks, core_copies):
        copy.wait_recv()
        own = grads[c, rows, :].astype(F32) + error[c, rows, :].astype(F32)
        pair[rows, :] = own + a_recv[rows, :]
        if step:
            s_copies.append(links.send(pair.at[rows], s_recv.at[step - 1], "x", step))

    def reducer(at, src, out, parts):
        made = []
        for number, (low, high, axes) in enumerate(parts):
            lanes = pl.ds(low, high - low)
            scratch = tuple(
                ref.at[at, :, :, lanes] for ref in (first,)
            ) + (mine.at[at, :, lanes], second.at[at, :, :, lanes], last.at[at, :, :, lanes])
            made.append(Reduce(links, src, out, lanes, axes, scratch))
        return stages(made)

    two = ((0, 512, "zyx"), (512, 1024, "yzx"))
    three = ((0, 384, "zyx"), (384, 768, "yxz"), (768, 1024, "xzy"))

    for low in range(0, N, 256):
        bufs[0, :, low : low + 256] = dot(proj_old[c], pair[:, low : low + 256], 0, 0)
    run_all(reducer(0, bufs.at[0], outs.at[0], two))
    for copy in s_copies:
        copy.wait_recv()
    total[...] = ((pair[rows_of(x, PIECE), :] + s_recv[0]) + s_recv[1]) + s_recv[2]

    wide1 = dot(outs[0], total[...], 1, 1)
    bufs[1] = dot(wide1, total[...])
    run_all(reducer(1, bufs.at[1], outs.at[1], three))

    size = jnp.sum(outs[0] * outs[1], axis=1, keepdims=True)
    scale = 1.0 / jnp.sqrt(size)
    normal[...] = outs[1] * scale
    wide2 = dot(normal[...], total[...], 1, 1)
    mine_lanes = rows_of(x, PIECE)
    wide[c, :, mine_lanes] = wide2
    own_block = wide.at[c, :, mine_lanes]
    wide_x = [links.send(own_block, own_block, "x", step) for step in (2, 1, 3)]
    wide_c = [links.send(own_block, own_block, "c", 1)]
    bufs[2] = dot(wide2, total[...])
    z_steps = reducer(2, bufs.at[2], summed.at[c], three)
    next(z_steps)
    for step, copy in zip((2, 1, 3), wide_x):
        copy.wait_recv()
        block = wide.at[c, :, rows_of(lax.rem(x - step + 4, 4), PIECE)]
        wide_c.append(links.send(block, block, "c", 1))

    def project(matrix):
        high, low = halves(wide[matrix])
        for at in range(0, N, 256):
            lanes = pl.ds(at, 256)
            g, e = grads[matrix, :, lanes], error[matrix, :, lanes]
            small = dot_bf16(low, g) + dot_bf16(low, e)
            ubuf[matrix, :, lanes] = (dot_bf16(high, g) + dot_bf16(high, e)) + small

    def local_reduce(matrix, axes, at):
        scratch = (ufirst.at[at], umine.at[at], usecond.at[at], None)
        return Reduce(links, ubuf.at[matrix], local.at[matrix], pl.ds(0, N), axes, scratch)

    project(c)
    own_part = local_reduce(c, "ab", 0)
    own_part.start()
    next(z_steps)
    for copy in wide_c:
        copy.wait_recv()
    project(other)
    other_part = local_reduce(other, "ba", 1)
    other_part.start()
    next(z_steps)
    work[:, :R] = dot(outs[0] * scale, normal[...], 1, 1)
    gram[...] = dot(normal[...], outs[0], 1, 1)
    inverse_factor(work)
    unmixed[...] = work[:, R:]
    next(z_steps)
    own_part.second_stage()
    other_part.second_stage()
    next(z_steps)
    own_part.third_stage()
    other_part.third_stage()
    own_part.gather_second()
    other_part.gather_second()
    next(z_steps)
    z_copy = links.send(summed.at[c], summed.at[c], "c", 1)
    own_part.gather_first()
    other_part.gather_first()
    columns = dot(unmixed[...], normal[...])
    crossed = dot(columns, summed[c], 1, 1)
    work[:, :R] = dot(crossed, unmixed[...], 1, 1)
    inverse_factor(work)
    mixer[c] = dot(work[:, R:], unmixed[...])
    m_copy = links.send(mixer.at[c], mixer.at[c], "c", 1)
    cross[c] = dot(mixer[c], gram[...])
    r_copy = links.send(cross.at[c], cross.at[c], "c", 1)
    own_part.wait()
    other_part.wait()
    z_copy.wait_recv()
    m_copy.wait_recv()
    r_copy.wait_recv()
    links.drain()


def final_kernel(
    grads, error, wide, local, summed, mixer, cross, moment1, moment2,
    update, error_new, proj_new, first_new, second_new,
):
    for k in range(2):
        mix = mixer[k]
        basis = dot(wide[k], mix, 0, 1)
        proj_new[k] = basis
        basis_high, basis_low = halves(basis)
        for at in range(0, N, 256):
            lanes = pl.ds(at, 256)
            projected = dot3(mix, local[k, :, lanes])
            high, low = halves(projected)
            back = dot_bf16(basis_high, high) + (
                dot_bf16(basis_high, low) + dot_bf16(basis_low, high)
            )
            accrued = grads[k, :, lanes].astype(F32) + error[k, :, lanes].astype(F32)
            error_new[k, :, lanes] = (accrued - back).astype(BF16)
            grad_proj = dot3(mix, summed[k, :, lanes]) / 8.0
            rotation = cross[k]
            m1, m2 = moment1[k, :, lanes], moment2[k, :, lanes]
            turned = dot3(rotation, m1)
            spread = jnp.abs(m2 - m1 * m1)
            spun = dot3(rotation * rotation, spread) + turned * turned
            one = 0.9 * turned + 0.1 * grad_proj
            two = 0.99 * spun + 0.01 * grad_proj * grad_proj
            first_new[k, :, lanes] = one
            second_new[k, :, lanes] = two
            high, low = halves(one / (jnp.sqrt(two) + 1e-06))
            moved = dot_bf16(basis_high, high) + (
                dot_bf16(basis_high, low) + dot_bf16(basis_low, high)
            )
            update[k, :, lanes] = moved.astype(BF16)


def on_device(grads, error, proj_old, moment1, moment2):
    grads, error = grads[0], error[0]
    vmem = pl.BlockSpec(memory_space=pltpu.VMEM)
    shape = jax.ShapeDtypeStruct
    wide, local, summed, mixer, cross = pl.pallas_call(
        main_kernel,
        out_shape=(
            shape((2, R, ROWS), F32),
            shape((2, R, N), F32),
            shape((2, R, N), F32),
            shape((2, R, R), F32),
            shape((2, R, R), F32),
        ),
        in_specs=[vmem] * 3,
        out_specs=(vmem,) * 5,
        scratch_shapes=[
            pltpu.VMEM((ROWS, N), F32),
            pltpu.VMEM((ROWS, N), F32),
            pltpu.VMEM((ROWS, N), F32),
            pltpu.VMEM((3, PIECE, N), F32),
            pltpu.VMEM((PIECE, N), F32),
            pltpu.VMEM((3, R, N), F32),
            pltpu.VMEM((2, R, N), F32),
            pltpu.VMEM((R, N), F32),
            pltpu.VMEM((R, 2 * R), F32),
            pltpu.VMEM((R, R), F32),
            pltpu.VMEM((R, R), F32),
            pltpu.VMEM((3, 3, 64, N), F32),
            pltpu.VMEM((3, 64, N), F32),
            pltpu.VMEM((3, 3, 16, N), F32),
            pltpu.VMEM((3, 4, 16, N), F32),
            pltpu.VMEM((2, 3, 64, N), F32),
            pltpu.VMEM((2, 64, N), F32),
            pltpu.VMEM((2, 3, 16, N), F32),
            pltpu.VMEM((2, R, N), F32),
            pltpu.SemaphoreType.DMA((COPIES,)),
            pltpu.SemaphoreType.DMA((COPIES,)),
        ],
        compiler_params=pltpu.CompilerParams(
            collective_id=0, has_side_effects=True, vmem_limit_bytes=50 * 1024 * 1024
        ),
    )(grads, error, proj_old)
    update, error_new, proj_new, first_new, second_new = pl.pallas_call(
        final_kernel,
        out_shape=(
            shape((2, ROWS, N), BF16),
            shape((2, ROWS, N), BF16),
            shape((2, ROWS, R), F32),
            shape((2, R, N), F32),
            shape((2, R, N), F32),
        ),
        in_specs=[vmem] * 9,
        out_specs=(vmem,) * 5,
        compiler_params=pltpu.CompilerParams(vmem_limit_bytes=50 * 1024 * 1024),
    )(grads, error, wide, local, summed, mixer, cross, moment1, moment2)
    return (update, error_new[None], proj_new, first_new, second_new)


def solution(mesh):
    in_specs = (
        P("dp", None, "fsdp", None),
        P("dp", None, "fsdp", None),
        P(None, "fsdp", None),
        P(),
        P(),
    )
    out_specs = (
        P(None, "fsdp", None),
        P("dp", None, "fsdp", None),
        P(None, "fsdp", None),
        P(),
        P(),
    )
    return jax.shard_map(
        on_device, mesh=mesh, in_specs=in_specs, out_specs=out_specs, check_vma=False
    )
```

```python
import functools
import jax
import jax.numpy as jnp
from jax import lax
from jax.experimental import pallas as pl
from jax.experimental.pallas import tpu as pltpu
from jax.sharding import PartitionSpec as P

F32 = jnp.float32
BF16 = jnp.bfloat16
MESH = pl.DeviceIdType.MESH
N = 1024
R = 256
ROWS = 512
PIECE = 128
BLOCK = 64
GROUP = 16
COPIES = 224
COLUMN_PARTS = ((0, 512, "zyx"), (512, 1024, "yzx"))
MIDDLE_PARTS = ((0, 384, "zyx"), (384, 768, "yxz"), (768, 1024, "xzy"))
LAST_PARTS = ((0, 256, "xzy"), (256, 512, "xyz"), (512, 768, "zyx"), (768, 1024, "yzx"))


def dot(a, b, ca=1, cb=0):
    return lax.dot_general(
        a,
        b,
        (((ca,), (cb,)), ((), ())),
        precision=lax.Precision.HIGHEST,
        preferred_element_type=F32,
    )


def halves(value):
    high = value.astype(BF16)
    return high, (value - high.astype(F32)).astype(BF16)


def dot_bf16(a, b, ca=1, cb=0):
    return lax.dot_general(a, b, (((ca,), (cb,)), ((), ())), preferred_element_type=F32)


def dot_halves(a, b, ca=1, cb=0):
    small = dot_bf16(a[0], b[1], ca, cb) + dot_bf16(a[1], b[0], ca, cb)
    return dot_bf16(a[0], b[0], ca, cb) + small


class Place:
    def __init__(self):
        dp, fsdp = lax.axis_index("dp"), lax.axis_index("fsdp")
        self.at = {
            "x": lax.div(dp, 2),
            "c": lax.rem(dp, 2),
            "y": lax.div(fsdp, 4),
            "z": lax.rem(fsdp, 4),
        }

    def peer(self, axis, step):
        new = dict(self.at)
        c = self.at["c"]
        if axis == "c":
            new["c"] = 1 - c
        elif axis == "a":
            new["z"] = lax.rem(new["z"] + (1 - c) * step, 4)
            new["y"] = lax.rem(new["y"] + c * step, 4)
        elif axis == "b":
            new["z"] = lax.rem(new["z"] + c * step, 4)
            new["y"] = lax.rem(new["y"] + (1 - c) * step, 4)
        else:
            new[axis] = lax.rem(new[axis] + step, 4)
        return (new["x"] * 2 + new["c"], new["y"] * 4 + new["z"])

    def index(self, axis):
        c, y, z = self.at["c"], self.at["y"], self.at["z"]
        if axis == "a":
            return z * (1 - c) + y * c
        if axis == "b":
            return y * (1 - c) + z * c
        return self.at[axis]


class Links:
    def __init__(self, place, send_sems, recv_sems):
        self.place, self.send_sems, self.recv_sems = place, send_sems, recv_sems
        self.used = 0
        self.started = []

    def send(self, src, dst, axis, step):
        at = self.used
        self.used += 1
        copy = pltpu.make_async_remote_copy(
            src_ref=src,
            dst_ref=dst,
            send_sem=self.send_sems.at[at],
            recv_sem=self.recv_sems.at[at],
            device_id=self.place.peer(axis, step),
            device_id_type=MESH,
        )
        copy.start()
        self.started.append(copy)
        return copy

    def drain(self):
        assert self.used <= COPIES
        for copy in self.started:
            copy.wait_send()


def rows_of(index, size):
    return pl.ds(pl.multiple_of(index * size, size), size)


class Reduce:
    def __init__(self, links, src, out, lanes, axes, scratch):
        self.links, self.src, self.out, self.lanes, self.axes = links, src, out, lanes, axes
        self.first, self.mine, self.second, self.last = scratch
        self.copies = None

    def start(self):
        axis = self.axes[0]
        me = self.links.place.index(axis)
        self.copies = []
        for step in (2, 1, 3):
            block = rows_of(lax.rem(me + step, 4), 64)
            self.copies.append(
                self.links.send(self.src.at[block, self.lanes], self.first.at[step - 1], axis, step)
            )

    def wait(self):
        for copy in self.copies:
            copy.wait_recv()

    def second_stage(self):
        self.wait()
        place = self.links.place
        me = place.index(self.axes[0])
        total = self.src[rows_of(me, 64), self.lanes]
        for slot in range(3):
            total = total + self.first[slot]
        self.mine[...] = total
        axis = self.axes[1]
        me = place.index(axis)
        self.copies = []
        for step in (2, 1, 3):
            block = rows_of(lax.rem(me + step, 4), 16)
            self.copies.append(
                self.links.send(self.mine.at[block], self.second.at[step - 1], axis, step)
            )

    def own_rows(self):
        place = self.links.place
        start = place.index(self.axes[0]) * 64 + place.index(self.axes[1]) * 16
        return pl.ds(pl.multiple_of(start, 16), 16)

    def third_stage(self):
        self.wait()
        place = self.links.place
        me = place.index(self.axes[1])
        total = self.mine[rows_of(me, 16)]
        for slot in range(3):
            total = total + self.second[slot]
        if len(self.axes) == 2:
            self.out[self.own_rows(), self.lanes] = total
            return
        axis = self.axes[2]
        me = place.index(axis)
        self.last[me] = total
        self.copies = []
        for step in (2, 1, 3):
            self.copies.append(self.links.send(self.last.at[me], self.last.at[me], axis, step))

    def gather_second(self):
        if len(self.axes) == 3:
            self.wait()
            self.out[self.own_rows(), self.lanes] = (
                (self.last[0] + self.last[1]) + (self.last[2] + self.last[3])
            )
        own = self.out.at[self.own_rows(), self.lanes]
        self.copies = [self.links.send(own, own, self.axes[1], step) for step in (2, 1, 3)]

    def gather_first(self):
        self.wait()
        axis = self.axes[0]
        own = self.out.at[rows_of(self.links.place.index(axis), 64), self.lanes]
        self.copies = [self.links.send(own, own, axis, step) for step in (2, 1, 3)]


class Ring:
    def __init__(self, links, axis, src, size, low, width, scratch):
        self.links, self.axis, self.src, self.size = links, axis, src, size
        self.via, self.sums, self.got = scratch
        self.half = half = width // 2
        self.lanes = pl.ds(low, width)
        self.left, self.right = pl.ds(low, half), pl.ds(low + half, half)
        self.copies = []

    def block(self, step):
        return rows_of(lax.rem(self.links.place.index(self.axis) + step, 4), self.size)

    def send(self, src, dst, step):
        copy = self.links.send(src, dst, self.axis, step)
        self.copies.append(copy)
        return copy

    def scatter_far(self):
        far = self.block(2)
        self.far = (
            self.links.send(self.src.at[far, self.left], self.via.at[0], self.axis, 1),
            self.links.send(self.src.at[far, self.right], self.via.at[1], self.axis, 3),
        )

    def scatter_next(self):
        self.send(
            self.src.at[self.block(1), self.right], self.got.at[0, :, pl.ds(self.half, self.half)], 1
        )

    def scatter_back(self):
        self.send(self.src.at[self.block(3), self.left], self.got.at[1, :, pl.ds(0, self.half)], 3)

    def relay(self):
        self.far[0].wait_recv()
        self.sums[0] = self.src[self.block(1), self.left] + self.via[0]
        self.send(self.sums.at[0], self.got.at[0, :, pl.ds(0, self.half)], 1)
        self.far[1].wait_recv()
        self.sums[1] = self.src[self.block(3), self.right] + self.via[1]
        self.send(self.sums.at[1], self.got.at[1, :, pl.ds(self.half, self.half)], 3)

    def collect(self):
        for copy in self.copies:
            copy.wait_recv()
        return (self.src[self.block(0), self.lanes] + self.got[0]) + self.got[1]

    def gather(self, out):
        own = out.at[self.block(0), self.lanes]
        self.copies = []
        self.send(own, own, 1)
        self.send(own, own, 3)

    def forward(self, out):
        right, left = self.copies
        self.copies = []
        right.wait_recv()
        part = out.at[self.block(3), self.left]
        self.send(part, part, 1)
        left.wait_recv()
        part = out.at[self.block(1), self.right]
        self.send(part, part, 3)

    def finish(self):
        for copy in self.copies:
            copy.wait_recv()


class Chunk:
    def __init__(self, links, axes, src, out, low, width, scratch):
        self.links, self.axes, self.out = links, axes, out
        self.mine, self.second = scratch[3:]
        self.ring = Ring(links, axes[0], src, 64, low, width, scratch[:3])
        self.lanes = pl.ds(low, width)

    def start(self):
        self.ring.scatter_far()
        self.ring.scatter_next()
        self.ring.scatter_back()

    def relay(self):
        self.ring.relay()

    def collect(self):
        self.mine[...] = self.ring.collect()
        axis = self.axes[1]
        me = self.links.place.index(axis)
        self.copies = []
        for step in (2, 1, 3):
            block = rows_of(lax.rem(me + step, 4), 16)
            self.copies.append(
                self.links.send(self.mine.at[block], self.second.at[step - 1], axis, step)
            )

    def spread(self):
        for copy in self.copies:
            copy.wait_recv()
        place = self.links.place
        me = place.index(self.axes[1])
        rows = pl.ds(pl.multiple_of(place.index(self.axes[0]) * 64 + me * 16, 16), 16)
        total = self.mine[rows_of(me, 16)]
        for slot in range(3):
            total = total + self.second[slot]
        self.out[rows, self.lanes] = total
        own = self.out.at[rows, self.lanes]
        self.copies = [self.links.send(own, own, self.axes[1], step) for step in (2, 1, 3)]

    def gather(self):
        for copy in self.copies:
            copy.wait_recv()
        self.ring.gather(self.out)

    def forward(self):
        self.ring.forward(self.out)

    def finish(self):
        self.ring.finish()


def stages(parts):
    for part in parts:
        part.second_stage()
    yield
    for part in parts:
        part.third_stage()
    yield
    for part in parts:
        part.gather_second()
    yield
    for part in parts:
        part.gather_first()
    yield
    for part in parts:
        part.wait()
    yield


def advance(steps, count):
    for _ in range(count):
        next(steps)


def eliminate(diag):
    lanes = lax.broadcasted_iota(jnp.int32, (8, 2 * BLOCK), 1)
    subs = lax.broadcasted_iota(jnp.int32, (8, 2 * BLOCK), 0)
    full = lambda value: jnp.broadcast_to(value, (8, 2 * BLOCK))
    count = BLOCK // 8
    state, pivots = [], []
    for v in range(count):
        block = jnp.concatenate([diag[8 * v : 8 * v + 8], jnp.zeros((8, BLOCK), F32)], axis=1)
        state.append(jnp.where(lanes == subs + (BLOCK + 8 * v), 1.0, block))
        pivots.append(None)
    for group in range(0, BLOCK, GROUP):
        columns = [
            [full(state[v][:, at : at + 1]) if v >= group // 8 else None for v in range(count)]
            for at in range(group, group + GROUP)
        ]
        for k in range(GROUP):
            here, sub = divmod(group + k, 8)
            pivot = full(columns[k][here][sub : sub + 1])
            inverse = 1.0 / pivot
            pivots[here] = pivot if sub == 0 else jnp.where(subs == sub, pivot, pivots[here])
            row = full(state[here][sub : sub + 1])
            heads = [full(columns[j][here][sub : sub + 1]) for j in range(k + 1, GROUP)]
            for v in range(here, count):
                factor = columns[k][v] * inverse
                if v == here:
                    factor = jnp.where(subs > sub, factor, 0.0)
                for j, head in zip(range(k + 1, GROUP), heads):
                    columns[j][v] = columns[j][v] - factor * head
                state[v] = state[v] - factor * row
    scaled = [state[v] * lax.rsqrt(pivots[v]) for v in range(count)]
    return jnp.concatenate(scaled, axis=0)[:, BLOCK:]


def factor_steps(work):
    rows = lax.broadcasted_iota(jnp.int32, (R, R), 0)
    lanes = lax.broadcasted_iota(jnp.int32, (R, R), 1)
    work[:, R:] = (rows == lanes).astype(F32)
    for block in range(R // BLOCK):
        low, high = block * BLOCK, (block + 1) * BLOCK
        scale = eliminate(work[low:high, low:high])
        yield
        strip = dot(scale, work[low:high, :])
        work[low:high, :] = strip
        if high < R:
            work[high:, :] = work[high:, :] - dot(strip[:, high:R], strip, 0, 0)
        yield


STOP = None


def main_kernel(
    grads_any, error_any, proj_any, wide, local, summed, mixer, cross, grads, error, proj_old,
    turned, a_send, a_recv, pair, s_via, s_sums, s_got, total, total_parts, bufs, outs, normal,
    work, gram, unmixed, first, mine, second, last, uvia, usums, ugot, umine, usecond, ubuf,
    in_sems, send_sems, recv_sems,
):
    place = Place()
    links = Links(place, send_sems, recv_sems)
    c, x = place.at["c"], place.at["x"]
    other = 1 - c
    order = (2, 1, 3, 0)
    blocks = [rows_of(lax.rem(x + step, 4), PIECE) for step in order]

    loads = []

    def load(source, target):
        copy = pltpu.make_async_copy(source, target, in_sems.at[len(loads)])
        copy.start()
        loads.append(copy)
        return copy

    def load_rows(matrix, rows):
        return [
            load(source.at[matrix, rows], target.at[matrix, rows])
            for source, target in ((grads_any, grads), (error_any, error))
        ]

    barrier = pltpu.get_barrier_semaphore()
    partners = [("c", 1)] + [(axis, step) for axis in "xyz" for step in (1, 2, 3)]
    for axis, step in partners:
        pl.semaphore_signal(barrier, inc=1, device_id=place.peer(axis, step), device_id_type=MESH)
    sent_loads = [load_rows(other, rows) for rows in blocks]
    proj_load = load(proj_any.at[c], proj_old)
    kept_loads = [load_rows(c, rows) for rows in blocks]

    for rows, copies in zip(blocks, sent_loads):
        for copy in copies:
            copy.wait()
        a_send[rows, :] = grads[other, rows, :].astype(F32) + error[other, rows, :].astype(F32)
    pl.semaphore_wait(barrier, len(partners))
    core_copies = [links.send(a_send.at[rows], a_recv.at[rows], "c", 1) for rows in blocks]
    proj_load.wait()
    turned[0], turned[1] = halves(proj_old[...].T)
    for rows, copies in zip(blocks, kept_loads):
        for copy in copies:
            copy.wait()
        pair[rows, :] = grads[c, rows, :].astype(F32) + error[c, rows, :].astype(F32)

    replicas = Ring(links, "x", pair, PIECE, 0, N, (s_via, s_sums, s_got))
    sends = (replicas.scatter_far, replicas.scatter_next, replicas.scatter_back, lambda: None)
    for at, (send, rows, copy) in enumerate(zip(sends, blocks, core_copies)):
        copy.wait_recv()
        pair[rows, :] = pair[rows, :] + a_recv[rows, :]
        send()
        left = (turned[0, :, rows], turned[1, :, rows])
        for low in range(0, N, 256):
            lanes = pl.ds(low, 256)
            piece = dot_halves(left, halves(pair[rows, lanes]))
            bufs[0, :, lanes] = piece if at == 0 else bufs[0, :, lanes] + piece

    def reducers(at, src, out, parts):
        made = []
        for low, high, axes in parts:
            lanes = pl.ds(low, high - low)
            scratch = (
                first.at[at, :, :, lanes],
                mine.at[at, :, lanes],
                second.at[at, :, :, lanes],
                last.at[at, :, :, lanes],
            )
            made.append(Reduce(links, src, out, lanes, axes, scratch))
        return made

    parts = reducers(0, bufs.at[0], outs.at[0], COLUMN_PARTS)
    for part in parts:
        part.start()
    steps = stages(parts)
    replicas.relay()
    advance(steps, 2)
    total[...] = replicas.collect()
    total_parts[0], total_parts[1] = halves(total[...])
    advance(steps, 3)
    if STOP == 1:
        return links.drain()

    def spread(at, wide_part, out, axes):
        made = reducers(at, bufs.at[at], out, axes)
        left = halves(wide_part)
        for part in made:
            lanes = part.lanes
            bufs[at, :, lanes] = dot_halves(left, (total_parts[0, :, lanes], total_parts[1, :, lanes]))
            part.start()
        return stages(made)

    def widen(columns):
        return dot_halves(halves(columns), (total_parts[0], total_parts[1]), 1, 1)

    steps = spread(1, widen(outs[0]), outs.at[1], MIDDLE_PARTS)
    advance(steps, 5)
    if STOP == 2:
        return links.drain()

    size = jnp.sum(outs[0] * outs[1], axis=1, keepdims=True)
    scale = 1.0 / jnp.sqrt(size)
    normal[...] = outs[1] * scale
    wide2 = widen(normal[...])
    mine_lanes = rows_of(x, PIECE)
    wide[c, :, mine_lanes] = wide2
    own_block = wide.at[c, :, mine_lanes]
    wide_x = [links.send(own_block, own_block, "x", step) for step in (2, 1, 3)]
    wide_c = [links.send(own_block, own_block, "c", 1)]
    z_steps = spread(2, wide2, summed.at[c], LAST_PARTS)

    work[:, :R] = dot(outs[0] * scale, normal[...], 1, 1)
    gram[...] = dot(normal[...], outs[0], 1, 1)
    factor = factor_steps(work)
    advance(factor, 3)
    for step, copy in zip((2, 1, 3), wide_x):
        copy.wait_recv()
        block = wide.at[c, :, rows_of(lax.rem(x - step + 4, 4), PIECE)]
        wide_c.append(links.send(block, block, "c", 1))
    next(z_steps)

    chunks = []
    width = N // 2

    def launch(matrix):
        high, small = halves(wide[matrix])
        for half, axes in ((0, "ab"), (1, "ba")):
            for low in range(half * width, (half + 1) * width, 256):
                lanes = pl.ds(low, 256)
                g, e = grads[matrix, :, lanes], error[matrix, :, lanes]
                rest = dot_bf16(small, g) + dot_bf16(small, e)
                ubuf[matrix, :, lanes] = (dot_bf16(high, g) + dot_bf16(high, e)) + rest
            at = len(chunks)
            scratch = (uvia.at[at], usums.at[at], ugot.at[at], umine.at[at], usecond.at[at])
            chunks.append(
                Chunk(
                    links, axes, ubuf.at[matrix], local.at[matrix], half * width, width, scratch
                )
            )
            chunks[-1].start()

    launch(c)
    next(z_steps)
    for copy in wide_c:
        copy.wait_recv()
    launch(other)
    early, late = chunks[:2], chunks[2:]
    advance(factor, 1)
    next(z_steps)
    for chunk in early:
        chunk.relay()
    advance(factor, 1)
    for chunk in late:
        chunk.relay()
    advance(factor, 3)
    unmixed[...] = work[:, R:]
    next(z_steps)
    for chunk in early:
        chunk.collect()
    columns = dot(unmixed[...], normal[...])
    for chunk in late:
        chunk.collect()
    for chunk in early:
        chunk.spread()
    for chunk in late:
        chunk.spread()
    for chunk in early:
        chunk.gather()
    next(z_steps)
    if STOP == 3:
        for chunk in late:
            chunk.gather()
        for chunk in chunks:
            chunk.forward()
        for chunk in chunks:
            chunk.finish()
        return links.drain()
    z_copy = links.send(summed.at[c], summed.at[c], "c", 1)

    crossed = dot(columns, summed[c], 1, 1)
    work[:, :R] = dot(crossed, unmixed[...], 1, 1)
    for chunk in late:
        chunk.gather()
    factor = factor_steps(work)
    advance(factor, 3)
    for chunk in early:
        chunk.forward()
    advance(factor, 2)
    for chunk in late:
        chunk.forward()
    advance(factor, 3)
    mixer[c] = dot(work[:, R:], unmixed[...])
    m_copy = links.send(mixer.at[c], mixer.at[c], "c", 1)
    cross[c] = dot(mixer[c], gram[...])
    r_copy = links.send(cross.at[c], cross.at[c], "c", 1)
    for chunk in chunks:
        chunk.finish()
    z_copy.wait_recv()
    m_copy.wait_recv()
    r_copy.wait_recv()
    links.drain()


def final_kernel(
    wide, mixer, local, grads, error, cross, summed, moment1, moment2,
    update, error_new, proj_new, first_new, second_new,
    v_wide, v_mixer, v_local, v_grads, v_error, v_cross, v_summed, v_moment1, v_moment2,
    v_update, v_error_new, v_proj_new, v_first_new, v_second_new, in_sems, out_sems,
):
    sources = (wide, mixer, local, grads, error, cross, summed, moment1, moment2)
    holds = (v_wide, v_mixer, v_local, v_grads, v_error, v_cross, v_summed, v_moment1, v_moment2)
    loads = []
    for k in range(2):
        made = [
            pltpu.make_async_copy(source.at[k], hold.at[k], in_sems.at[k, at])
            for at, (source, hold) in enumerate(zip(sources, holds))
        ]
        for copy in made:
            copy.start()
        loads.append(made)
    stores = []

    def store(hold, result, k, at):
        copy = pltpu.make_async_copy(hold.at[k], result.at[k], out_sems.at[k, at])
        copy.start()
        stores.append(copy)

    for k in range(2):
        loads[k][0].wait()
        loads[k][1].wait()
        mix = v_mixer[k]
        basis = dot(v_wide[k], mix, 0, 1)
        v_proj_new[k] = basis
        store(v_proj_new, proj_new, k, 2)
        basis, mix = halves(basis), halves(mix)
        for at in range(2, 9):
            loads[k][at].wait()
        rotation = v_cross[k]
        turn, spin = halves(rotation), halves(rotation * rotation)
        for at in range(0, N, 256):
            lanes = pl.ds(at, 256)
            projected = dot_halves(mix, halves(v_local[k, :, lanes]))
            back = dot_halves(basis, halves(projected))
            accrued = v_grads[k, :, lanes].astype(F32) + v_error[k, :, lanes].astype(F32)
            v_error_new[k, :, lanes] = (accrued - back).astype(BF16)
            grad_proj = dot_halves(mix, halves(v_summed[k, :, lanes])) / 8.0
            m1, m2 = v_moment1[k, :, lanes], v_moment2[k, :, lanes]
            turned = dot_halves(turn, halves(m1))
            spun = dot_halves(spin, halves(jnp.abs(m2 - m1 * m1)))
            one = 0.9 * turned + 0.1 * grad_proj
            two = 0.99 * (spun + turned * turned) + 0.01 * grad_proj * grad_proj
            v_first_new[k, :, lanes] = one
            v_second_new[k, :, lanes] = two
            step = one / (jnp.sqrt(two) + 1e-06)
            v_update[k, :, lanes] = dot_halves(basis, halves(step)).astype(BF16)
        store(v_error_new, error_new, k, 1)
        store(v_first_new, first_new, k, 3)
        store(v_second_new, second_new, k, 4)
        store(v_update, update, k, 0)
    for copy in stores:
        copy.wait()


def on_device(grads, error, proj_old, moment1, moment2):
    grads, error = grads[0], error[0]
    vmem = pl.BlockSpec(memory_space=pltpu.VMEM)
    anywhere = pl.BlockSpec(memory_space=pl.ANY)
    shape = jax.ShapeDtypeStruct
    wide, local, summed, mixer, cross = pl.pallas_call(
        main_kernel,
        out_shape=(
            shape((2, R, ROWS), F32),
            shape((2, R, N), F32),
            shape((2, R, N), F32),
            shape((2, R, R), F32),
            shape((2, R, R), F32),
        ),
        in_specs=[anywhere] * 3,
        out_specs=(vmem,) * 5,
        scratch_shapes=[
            pltpu.VMEM((2, ROWS, N), BF16),
            pltpu.VMEM((2, ROWS, N), BF16),
            pltpu.VMEM((ROWS, R), F32),
            pltpu.VMEM((2, R, ROWS), BF16),
            pltpu.VMEM((ROWS, N), F32),
            pltpu.VMEM((ROWS, N), F32),
            pltpu.VMEM((ROWS, N), F32),
            pltpu.VMEM((2, PIECE, N // 2), F32),
            pltpu.VMEM((2, PIECE, N // 2), F32),
            pltpu.VMEM((2, PIECE, N), F32),
            pltpu.VMEM((PIECE, N), F32),
            pltpu.VMEM((2, PIECE, N), BF16),
            pltpu.VMEM((3, R, N), F32),
            pltpu.VMEM((2, R, N), F32),
            pltpu.VMEM((R, N), F32),
            pltpu.VMEM((R, 2 * R), F32),
            pltpu.VMEM((R, R), F32),
            pltpu.VMEM((R, R), F32),
            pltpu.VMEM((3, 3, 64, N), F32),
            pltpu.VMEM((3, 64, N), F32),
            pltpu.VMEM((3, 3, 16, N), F32),
            pltpu.VMEM((3, 4, 16, N), F32),
            pltpu.VMEM((4, 2, 64, N // 4), F32),
            pltpu.VMEM((4, 2, 64, N // 4), F32),
            pltpu.VMEM((4, 2, 64, N // 2), F32),
            pltpu.VMEM((4, 64, N // 2), F32),
            pltpu.VMEM((4, 3, 16, N // 2), F32),
            pltpu.VMEM((2, R, N), F32),
            pltpu.SemaphoreType.DMA((17,)),
            pltpu.SemaphoreType.DMA((COPIES,)),
            pltpu.SemaphoreType.DMA((COPIES,)),
        ],
        compiler_params=pltpu.CompilerParams(
            collective_id=0, has_side_effects=True, vmem_limit_bytes=50 * 1024 * 1024
        ),
    )(grads, error, proj_old)
    inputs = (wide, mixer, local, grads, error, cross, summed, moment1, moment2)
    outputs = (
        shape((2, ROWS, N), BF16),
        shape((2, ROWS, N), BF16),
        shape((2, ROWS, R), F32),
        shape((2, R, N), F32),
        shape((2, R, N), F32),
    )
    update, error_new, proj_new, first_new, second_new = pl.pallas_call(
        final_kernel,
        out_shape=outputs,
        in_specs=[anywhere] * 9,
        out_specs=(anywhere,) * 5,
        scratch_shapes=[pltpu.VMEM(one.shape, one.dtype) for one in inputs + outputs]
        + [pltpu.SemaphoreType.DMA((2, 9)), pltpu.SemaphoreType.DMA((2, 5))],
        compiler_params=pltpu.CompilerParams(vmem_limit_bytes=50 * 1024 * 1024),
    )(*inputs)
    return (update, error_new[None], proj_new, first_new, second_new)


def solution(mesh):
    in_specs = (
        P("dp", None, "fsdp", None),
        P("dp", None, "fsdp", None),
        P(None, "fsdp", None),
        P(),
        P(),
    )
    out_specs = (
        P(None, "fsdp", None),
        P("dp", None, "fsdp", None),
        P(None, "fsdp", None),
        P(),
        P(),
    )
    return jax.shard_map(
        on_device, mesh=mesh, in_specs=in_specs, out_specs=out_specs, check_vma=False
    )
```

```python
import functools
import jax
import jax.numpy as jnp
from jax import lax
from jax.experimental import pallas as pl
from jax.experimental.pallas import tpu as pltpu
from jax.sharding import PartitionSpec as P

F32 = jnp.float32
BF16 = jnp.bfloat16
MESH = pl.DeviceIdType.MESH
N = 1024
R = 256
ROWS = 512
PIECE = 128
BLOCK = 64
GROUP = 16
COPIES = 160
CUTS = 2
COLUMN_PARTS = ((0, 512, "zyx"), (512, 1024, "yzx"))
MIDDLE_PARTS = ((0, 384, "zyx"), (384, 768, "yxz"), (768, 1024, "xzy"))
LAST_PARTS = ((0, 256, "xzy"), (256, 512, "xyz"), (512, 768, "zyx"), (768, 1024, "yzx"))


def dot(a, b, ca=1, cb=0):
    return lax.dot_general(
        a,
        b,
        (((ca,), (cb,)), ((), ())),
        precision=lax.Precision.HIGHEST,
        preferred_element_type=F32,
    )


def halves(value):
    high = value.astype(BF16)
    return high, (value - high.astype(F32)).astype(BF16)


def dot_bf16(a, b, ca=1, cb=0):
    return lax.dot_general(a, b, (((ca,), (cb,)), ((), ())), preferred_element_type=F32)


def dot_halves(a, b, ca=1, cb=0):
    small = dot_bf16(a[0], b[1], ca, cb) + dot_bf16(a[1], b[0], ca, cb)
    return dot_bf16(a[0], b[0], ca, cb) + small


class Place:
    def __init__(self):
        dp, fsdp = lax.axis_index("dp"), lax.axis_index("fsdp")
        self.at = {
            "x": lax.div(dp, 2),
            "c": lax.rem(dp, 2),
            "y": lax.div(fsdp, 4),
            "z": lax.rem(fsdp, 4),
        }

    def peer(self, axis, step):
        new = dict(self.at)
        c = self.at["c"]
        if axis == "c":
            new["c"] = 1 - c
        elif axis == "a":
            new["z"] = lax.rem(new["z"] + (1 - c) * step, 4)
            new["y"] = lax.rem(new["y"] + c * step, 4)
        elif axis == "b":
            new["z"] = lax.rem(new["z"] + c * step, 4)
            new["y"] = lax.rem(new["y"] + (1 - c) * step, 4)
        else:
            new[axis] = lax.rem(new[axis] + step, 4)
        return (new["x"] * 2 + new["c"], new["y"] * 4 + new["z"])

    def index(self, axis):
        c, y, z = self.at["c"], self.at["y"], self.at["z"]
        if axis == "a":
            return z * (1 - c) + y * c
        if axis == "b":
            return y * (1 - c) + z * c
        return self.at[axis]


class Links:
    def __init__(self, place, send_sems, recv_sems):
        self.place, self.send_sems, self.recv_sems = place, send_sems, recv_sems
        self.used = 0
        self.started = []

    def slot(self):
        at = self.used
        self.used += 1
        return at

    def copy(self, src, dst, axis, step, at):
        return pltpu.make_async_remote_copy(
            src_ref=src,
            dst_ref=dst,
            send_sem=self.send_sems.at[at],
            recv_sem=self.recv_sems.at[at],
            device_id=self.place.peer(axis, step),
            device_id_type=MESH,
        )

    def send(self, src, dst, axis, step):
        copy = self.copy(src, dst, axis, step, self.slot())
        copy.start()
        self.started.append(copy)
        return copy

    def drain(self):
        assert self.used <= COPIES
        for copy in self.started:
            copy.wait_send()


class Group:
    def __init__(self, links, whole):
        self.links, self.at = links, links.slot()
        self.all = links.copy(whole, whole, "c", 1, self.at)
        links.started.append(self.all)

    def send(self, src, dst, axis, step):
        self.links.copy(src, dst, axis, step, self.at).start()

    def wait(self):
        self.all.wait_recv()


def rows_of(index, size):
    return pl.ds(pl.multiple_of(index * size, size), size)


class Reduce:
    def __init__(self, links, src, out, base, rows, lanes, axes, scratch):
        self.links, self.src, self.out, self.lanes, self.axes = links, src, out, lanes, axes
        self.base, self.large, self.small = base, rows // 4, rows // 16
        self.first, self.mine, self.second, self.last = scratch
        self.group = None

    def large_rows(self, index):
        return pl.ds(pl.multiple_of(self.base + index * self.large, 8), self.large)

    def small_rows(self, index):
        return pl.ds(pl.multiple_of(index * self.small, 8), self.small)

    def start(self):
        axis = self.axes[0]
        me = self.links.place.index(axis)
        self.group = Group(self.links, self.first)
        for step in (2, 1, 3):
            block = self.large_rows(lax.rem(me + step, 4))
            self.group.send(self.src.at[block, self.lanes], self.first.at[step - 1], axis, step)

    def wait(self):
        self.group.wait()

    def second_stage(self):
        self.wait()
        place = self.links.place
        total = self.src[self.large_rows(place.index(self.axes[0])), self.lanes]
        for slot in range(3):
            total = total + self.first[slot]
        self.mine[...] = total
        axis = self.axes[1]
        me = place.index(axis)
        self.group = Group(self.links, self.second)
        for step in (2, 1, 3):
            block = self.small_rows(lax.rem(me + step, 4))
            self.group.send(self.mine.at[block], self.second.at[step - 1], axis, step)

    def own_rows(self):
        place = self.links.place
        start = place.index(self.axes[0]) * self.large + place.index(self.axes[1]) * self.small
        return pl.ds(pl.multiple_of(self.base + start, 8), self.small)

    def third_stage(self):
        self.wait()
        place = self.links.place
        total = self.mine[self.small_rows(place.index(self.axes[1]))]
        for slot in range(3):
            total = total + self.second[slot]
        if len(self.axes) == 2:
            self.out[self.own_rows(), self.lanes] = total
            return
        axis = self.axes[2]
        me = place.index(axis)
        self.last[me] = total
        self.group = Group(self.links, self.last.at[pl.ds(0, 3)])
        for step in (2, 1, 3):
            self.group.send(self.last.at[me], self.last.at[me], axis, step)

    def gather_second(self):
        if len(self.axes) == 3:
            self.wait()
            self.out[self.own_rows(), self.lanes] = (
                (self.last[0] + self.last[1]) + (self.last[2] + self.last[3])
            )
        own = self.out.at[self.own_rows(), self.lanes]
        self.group = Group(self.links, self.second)
        for step in (2, 1, 3):
            self.group.send(own, own, self.axes[1], step)

    def gather_first(self):
        self.wait()
        axis = self.axes[0]
        own = self.out.at[self.large_rows(self.links.place.index(axis)), self.lanes]
        self.group = Group(self.links, self.first)
        for step in (2, 1, 3):
            self.group.send(own, own, axis, step)


class Ring:
    def __init__(self, links, axis, src, size, low, width, scratch):
        self.links, self.axis, self.src, self.size = links, axis, src, size
        self.via, self.sums, self.got = scratch
        self.half = half = width // 2
        self.lanes = pl.ds(low, width)
        self.left, self.right = pl.ds(low, half), pl.ds(low + half, half)

    def block(self, step):
        return rows_of(lax.rem(self.links.place.index(self.axis) + step, 4), self.size)

    def scatter_far(self):
        far = self.block(2)
        self.far = (
            self.links.send(self.src.at[far, self.left], self.via.at[0], self.axis, 1),
            self.links.send(self.src.at[far, self.right], self.via.at[1], self.axis, 3),
        )
        self.groups = Group(self.links, self.got.at[0]), Group(self.links, self.got.at[1])

    def scatter_next(self):
        target = self.got.at[0, :, pl.ds(self.half, self.half)]
        self.groups[0].send(self.src.at[self.block(1), self.right], target, self.axis, 1)

    def scatter_back(self):
        target = self.got.at[1, :, pl.ds(0, self.half)]
        self.groups[1].send(self.src.at[self.block(3), self.left], target, self.axis, 3)

    def relay(self):
        self.far[0].wait_recv()
        self.sums[0] = self.src[self.block(1), self.left] + self.via[0]
        target = self.got.at[0, :, pl.ds(0, self.half)]
        self.groups[0].send(self.sums.at[0], target, self.axis, 1)
        self.far[1].wait_recv()
        self.sums[1] = self.src[self.block(3), self.right] + self.via[1]
        target = self.got.at[1, :, pl.ds(self.half, self.half)]
        self.groups[1].send(self.sums.at[1], target, self.axis, 3)

    def collect(self):
        self.groups[0].wait()
        self.groups[1].wait()
        return (self.src[self.block(0), self.lanes] + self.got[0]) + self.got[1]

    def gather(self, out):
        own = out.at[self.block(0), self.lanes]
        self.copies = [self.links.send(own, own, self.axis, step) for step in (1, 3)]

    def forward(self, out):
        self.group = Group(self.links, self.got.at[0])
        self.copies[0].wait_recv()
        part = out.at[self.block(3), self.left]
        self.group.send(part, part, self.axis, 1)
        self.copies[1].wait_recv()
        part = out.at[self.block(1), self.right]
        self.group.send(part, part, self.axis, 3)

    def finish(self):
        self.group.wait()


class Chunk:
    def __init__(self, links, axes, src, out, low, width, scratch):
        self.links, self.axes, self.out = links, axes, out
        self.mine, self.second = scratch[3:]
        self.ring = Ring(links, axes[0], src, 64, low, width, scratch[:3])
        self.lanes = pl.ds(low, width)

    def start(self):
        self.ring.scatter_far()
        self.ring.scatter_next()
        self.ring.scatter_back()

    def relay(self):
        self.ring.relay()

    def collect(self):
        self.mine[...] = self.ring.collect()
        axis = self.axes[1]
        me = self.links.place.index(axis)
        self.group = Group(self.links, self.second)
        for step in (2, 1, 3):
            block = rows_of(lax.rem(me + step, 4), 16)
            self.group.send(self.mine.at[block], self.second.at[step - 1], axis, step)

    def spread(self):
        self.group.wait()
        place = self.links.place
        me = place.index(self.axes[1])
        rows = pl.ds(pl.multiple_of(place.index(self.axes[0]) * 64 + me * 16, 16), 16)
        total = self.mine[rows_of(me, 16)]
        for slot in range(3):
            total = total + self.second[slot]
        self.out[rows, self.lanes] = total
        own = self.out.at[rows, self.lanes]
        self.group = Group(self.links, self.second)
        for step in (2, 1, 3):
            self.group.send(own, own, self.axes[1], step)

    def gather(self):
        self.group.wait()
        self.ring.gather(self.out)

    def forward(self):
        self.ring.forward(self.out)

    def finish(self):
        self.ring.finish()


def stages(parts):
    for part in parts:
        part.second_stage()
    yield
    for part in parts:
        part.third_stage()
    yield
    for part in parts:
        part.gather_second()
    yield
    for part in parts:
        part.gather_first()
    yield
    for part in parts:
        part.wait()
    yield


def advance(steps, count):
    for _ in range(count):
        next(steps)


def eliminate(diag):
    lanes = lax.broadcasted_iota(jnp.int32, (8, 2 * BLOCK), 1)
    subs = lax.broadcasted_iota(jnp.int32, (8, 2 * BLOCK), 0)
    full = lambda value: jnp.broadcast_to(value, (8, 2 * BLOCK))
    count = BLOCK // 8
    state, pivots = [], []
    for v in range(count):
        block = jnp.concatenate([diag[8 * v : 8 * v + 8], jnp.zeros((8, BLOCK), F32)], axis=1)
        state.append(jnp.where(lanes == subs + (BLOCK + 8 * v), 1.0, block))
        pivots.append(None)
    for group in range(0, BLOCK, GROUP):
        columns = [
            [full(state[v][:, at : at + 1]) if v >= group // 8 else None for v in range(count)]
            for at in range(group, group + GROUP)
        ]
        for k in range(GROUP):
            here, sub = divmod(group + k, 8)
            pivot = full(columns[k][here][sub : sub + 1])
            inverse = 1.0 / pivot
            pivots[here] = pivot if sub == 0 else jnp.where(subs == sub, pivot, pivots[here])
            row = full(state[here][sub : sub + 1])
            heads = [full(columns[j][here][sub : sub + 1]) for j in range(k + 1, GROUP)]
            for v in range(here, count):
                factor = columns[k][v] * inverse
                if v == here:
                    factor = jnp.where(subs > sub, factor, 0.0)
                for j, head in zip(range(k + 1, GROUP), heads):
                    columns[j][v] = columns[j][v] - factor * head
                state[v] = state[v] - factor * row
    scaled = [state[v] * lax.rsqrt(pivots[v]) for v in range(count)]
    return jnp.concatenate(scaled, axis=0)[:, BLOCK:]


def factor_steps(work):
    rows = lax.broadcasted_iota(jnp.int32, (R, R), 0)
    lanes = lax.broadcasted_iota(jnp.int32, (R, R), 1)
    work[:, R:] = (rows == lanes).astype(F32)
    for block in range(R // BLOCK):
        low, high = block * BLOCK, (block + 1) * BLOCK
        scale = eliminate(work[low:high, low:high])
        yield
        strip = dot(scale, work[low:high, :])
        work[low:high, :] = strip
        if high < R:
            work[high:, :] = work[high:, :] - dot(strip[:, high:R], strip, 0, 0)
        yield


def main_kernel(
    grads_any, error_any, proj_any, wide, local, summed, mixer, cross, grads, error, proj_old,
    turned, a_send, a_recv, pair, s_via, s_sums, s_got, total, total_parts, bufs, outs, normal,
    work, gram, unmixed, first, mine, second, last, uvia, usums, ugot, umine, usecond, ubuf,
    grams, gfirst, gmine, gsecond, in_sems, send_sems, recv_sems,
):
    place = Place()
    links = Links(place, send_sems, recv_sems)
    c, x = place.at["c"], place.at["x"]
    other = 1 - c
    order = (2, 1, 3, 0)
    blocks = [rows_of(lax.rem(x + step, 4), PIECE) for step in order]

    loads = []

    def load(source, target):
        copy = pltpu.make_async_copy(source, target, in_sems.at[len(loads)])
        copy.start()
        loads.append(copy)
        return copy

    def load_rows(matrix, rows):
        return [
            load(source.at[matrix, rows], target.at[matrix, rows])
            for source, target in ((grads_any, grads), (error_any, error))
        ]

    barrier = pltpu.get_barrier_semaphore()
    partners = [("c", 1)] + [(axis, step) for axis in "xyz" for step in (1, 2, 3)]
    for axis, step in partners:
        pl.semaphore_signal(barrier, inc=1, device_id=place.peer(axis, step), device_id_type=MESH)
    sent_loads = [load_rows(other, rows) for rows in blocks]
    proj_load = load(proj_any.at[c], proj_old)
    kept_loads = [load_rows(c, rows) for rows in blocks]

    for rows, copies in zip(blocks, sent_loads):
        for copy in copies:
            copy.wait()
        a_send[rows, :] = grads[other, rows, :].astype(F32) + error[other, rows, :].astype(F32)
    pl.semaphore_wait(barrier, len(partners))
    core_copies = [links.send(a_send.at[rows], a_recv.at[rows], "c", 1) for rows in blocks]
    proj_load.wait()
    turned[0], turned[1] = halves(proj_old[...].T)
    for rows, copies in zip(blocks, kept_loads):
        for copy in copies:
            copy.wait()
        pair[rows, :] = grads[c, rows, :].astype(F32) + error[c, rows, :].astype(F32)

    replicas = Ring(links, "x", pair, PIECE, 0, N, (s_via, s_sums, s_got))
    sends = (replicas.scatter_far, replicas.scatter_next, replicas.scatter_back, lambda: None)
    for at, (send, rows, copy) in enumerate(zip(sends, blocks, core_copies)):
        copy.wait_recv()
        pair[rows, :] = pair[rows, :] + a_recv[rows, :]
        send()
        left = (turned[0, :, rows], turned[1, :, rows])
        for low in range(0, N, 256):
            lanes = pl.ds(low, 256)
            piece = dot_halves(left, halves(pair[rows, lanes]))
            bufs[0, :, lanes] = piece if at == 0 else bufs[0, :, lanes] + piece

    def reducers(at, src, out, parts, cuts):
        made = []
        rows = R // cuts
        for cut in range(cuts):
            large, small = pl.ds(cut * rows // 4, rows // 4), pl.ds(cut * rows // 16, rows // 16)
            for low, high, axes in parts:
                lanes = pl.ds(low, high - low)
                scratch = (
                    first.at[at, :, large, lanes],
                    mine.at[at, large, lanes],
                    second.at[at, :, small, lanes],
                    last.at[at, :, small, lanes],
                )
                made.append(Reduce(links, src, out, cut * rows, rows, lanes, axes, scratch))
        return made

    parts = reducers(0, bufs.at[0], outs.at[0], COLUMN_PARTS, CUTS)
    for part in parts:
        part.start()
    steps = stages(parts)
    replicas.relay()
    advance(steps, 2)
    own_total = replicas.collect()
    total[rows_of(x, PIECE), :] = own_total
    replicas.gather(total)
    total_parts[0, rows_of(x, PIECE)], total_parts[1, rows_of(x, PIECE)] = halves(own_total)
    advance(steps, 3)
    def spread(at, wide_part, out, axes, cuts):
        made = reducers(at, bufs.at[at], out, axes, cuts)
        left = halves(wide_part)
        own = rows_of(x, PIECE)
        for low, high, _ in axes:
            lanes = pl.ds(low, high - low)
            bufs[at, :, lanes] = dot_halves(
                left, (total_parts[0, own, lanes], total_parts[1, own, lanes])
            )
        for part in made:
            part.start()
        return stages(made)

    def widen(columns, rows):
        return dot_halves(
            halves(columns), (total_parts[0, rows], total_parts[1, rows]), 1, 1
        )

    steps = spread(1, widen(outs[0], rows_of(x, PIECE)), outs.at[1], MIDDLE_PARTS, CUTS)
    replicas.forward(total)
    for step in (1, 3):
        rows = replicas.block(step)
        total_parts[0, rows], total_parts[1, rows] = halves(total[rows])
    advance(steps, 5)
    replicas.finish()
    rows = replicas.block(2)
    total_parts[0, rows], total_parts[1, rows] = halves(total[rows])
    size = jnp.sum(outs[0] * outs[1], axis=1, keepdims=True)
    scale = 1.0 / jnp.sqrt(size)
    normal[...] = outs[1] * scale
    wide[c] = widen(normal[...], pl.ds(0, ROWS))
    wide_copy = links.send(wide.at[c], wide.at[c], "c", 1)
    grams[0] = dot(wide[c], wide[c], 1, 1)
    gram_parts = []
    for low, axes in ((0, "zy"), (128, "yz")):
        lanes = pl.ds(low, 128)
        scratch = (gfirst.at[:, :, lanes], gmine.at[:, lanes], gsecond.at[:, :, lanes], None)
        gram_parts.append(Reduce(links, grams.at[0], grams.at[1], 0, R, lanes, axes, scratch))
    for part in gram_parts:
        part.start()
    g_steps = stages(gram_parts)

    chunks = []
    width = N // 2

    def launch(matrix):
        high, small = halves(wide[matrix])
        for half, axes in ((0, "ab"), (1, "ba")):
            for low in range(half * width, (half + 1) * width, 256):
                lanes = pl.ds(low, 256)
                g, e = grads[matrix, :, lanes], error[matrix, :, lanes]
                rest = dot_bf16(small, g) + dot_bf16(small, e)
                ubuf[matrix, :, lanes] = (dot_bf16(high, g) + dot_bf16(high, e)) + rest
            at = len(chunks)
            scratch = (uvia.at[at], usums.at[at], ugot.at[at], umine.at[at], usecond.at[at])
            chunks.append(
                Chunk(
                    links, axes, ubuf.at[matrix], local.at[matrix], half * width, width, scratch
                )
            )
            chunks[-1].start()

    launch(c)
    work[:, :R] = dot(outs[0] * scale, normal[...], 1, 1)
    wide_copy.wait_recv()
    next(g_steps)
    launch(other)
    early, late = chunks[:2], chunks[2:]
    z_steps = spread(2, wide[c, :, rows_of(x, PIECE)], summed.at[c], LAST_PARTS, 1)
    factor = factor_steps(work)
    advance(factor, 1)
    advance(g_steps, 2)
    for chunk in early:
        chunk.relay()
    advance(factor, 1)
    for chunk in late:
        chunk.relay()
    advance(factor, 1)
    next(g_steps)
    for chunk in early:
        chunk.collect()
    advance(factor, 2)
    for chunk in late:
        chunk.collect()
    advance(factor, 1)
    next(z_steps)
    for chunk in early:
        chunk.spread()
    advance(factor, 2)
    unmixed[...] = work[:, R:]
    next(z_steps)
    for chunk in late:
        chunk.spread()
    next(g_steps)
    work[:, :R] = dot(dot(unmixed[...], grams[1]), unmixed[...], 1, 1)
    factor = factor_steps(work)
    advance(factor, 1)
    for chunk in early:
        chunk.gather()
    next(z_steps)
    advance(factor, 1)
    for chunk in late:
        chunk.gather()
    advance(factor, 1)
    next(z_steps)
    gram[...] = dot(normal[...], outs[0], 1, 1)
    advance(factor, 1)
    for chunk in early:
        chunk.forward()
    advance(factor, 2)
    for chunk in late:
        chunk.forward()
    advance(factor, 2)
    mixer[c] = dot(work[:, R:], unmixed[...])
    m_copy = links.send(mixer.at[c], mixer.at[c], "c", 1)
    cross[c] = dot(mixer[c], gram[...])
    r_copy = links.send(cross.at[c], cross.at[c], "c", 1)
    next(z_steps)
    z_copy = links.send(summed.at[c], summed.at[c], "c", 1)
    for chunk in chunks:
        chunk.finish()
    z_copy.wait_recv()
    m_copy.wait_recv()
    r_copy.wait_recv()
    links.drain()


def final_kernel(
    wide, mixer, local, grads, error, cross, summed, moment1, moment2,
    update, error_new, proj_new, first_new, second_new,
    v_wide, v_mixer, v_local, v_grads, v_error, v_cross, v_summed, v_moment1, v_moment2,
    v_update, v_error_new, v_proj_new, v_first_new, v_second_new, in_sems, out_sems,
):
    sources = (wide, mixer, local, grads, error, cross, summed, moment1, moment2)
    holds = (v_wide, v_mixer, v_local, v_grads, v_error, v_cross, v_summed, v_moment1, v_moment2)
    loads = []
    for k in range(2):
        made = [
            pltpu.make_async_copy(source.at[k], hold.at[k], in_sems.at[k, at])
            for at, (source, hold) in enumerate(zip(sources, holds))
        ]
        for copy in made:
            copy.start()
        loads.append(made)
    stores = []

    def store(hold, result, k, at):
        copy = pltpu.make_async_copy(hold.at[k], result.at[k], out_sems.at[k, at])
        copy.start()
        stores.append(copy)

    for k in range(2):
        loads[k][0].wait()
        loads[k][1].wait()
        mix = v_mixer[k]
        basis = dot(v_wide[k], mix, 0, 1)
        v_proj_new[k] = basis
        store(v_proj_new, proj_new, k, 2)
        basis, mix = halves(basis), halves(mix)
        for at in range(2, 9):
            loads[k][at].wait()
        rotation = v_cross[k]
        turn, spin = halves(rotation), halves(rotation * rotation)
        for at in range(0, N, 256):
            lanes = pl.ds(at, 256)
            projected = dot_halves(mix, halves(v_local[k, :, lanes]))
            back = dot_halves(basis, halves(projected))
            accrued = v_grads[k, :, lanes].astype(F32) + v_error[k, :, lanes].astype(F32)
            v_error_new[k, :, lanes] = (accrued - back).astype(BF16)
            grad_proj = dot_halves(mix, halves(v_summed[k, :, lanes])) / 8.0
            m1, m2 = v_moment1[k, :, lanes], v_moment2[k, :, lanes]
            turned = dot_halves(turn, halves(m1))
            spun = dot_halves(spin, halves(jnp.abs(m2 - m1 * m1)))
            one = 0.9 * turned + 0.1 * grad_proj
            two = 0.99 * (spun + turned * turned) + 0.01 * grad_proj * grad_proj
            v_first_new[k, :, lanes] = one
            v_second_new[k, :, lanes] = two
            step = one / (jnp.sqrt(two) + 1e-06)
            v_update[k, :, lanes] = dot_halves(basis, halves(step)).astype(BF16)
        store(v_error_new, error_new, k, 1)
        store(v_first_new, first_new, k, 3)
        store(v_second_new, second_new, k, 4)
        store(v_update, update, k, 0)
    for copy in stores:
        copy.wait()


def on_device(grads, error, proj_old, moment1, moment2):
    grads, error = grads[0], error[0]
    vmem = pl.BlockSpec(memory_space=pltpu.VMEM)
    anywhere = pl.BlockSpec(memory_space=pl.ANY)
    shape = jax.ShapeDtypeStruct
    wide, local, summed, mixer, cross = pl.pallas_call(
        main_kernel,
        out_shape=(
            shape((2, R, ROWS), F32),
            shape((2, R, N), F32),
            shape((2, R, N), F32),
            shape((2, R, R), F32),
            shape((2, R, R), F32),
        ),
        in_specs=[anywhere] * 3,
        out_specs=(vmem,) * 5,
        scratch_shapes=[
            pltpu.VMEM((2, ROWS, N), BF16),
            pltpu.VMEM((2, ROWS, N), BF16),
            pltpu.VMEM((ROWS, R), F32),
            pltpu.VMEM((2, R, ROWS), BF16),
            pltpu.VMEM((ROWS, N), F32),
            pltpu.VMEM((ROWS, N), F32),
            pltpu.VMEM((ROWS, N), F32),
            pltpu.VMEM((2, PIECE, N // 2), F32),
            pltpu.VMEM((2, PIECE, N // 2), F32),
            pltpu.VMEM((2, PIECE, N), F32),
            pltpu.VMEM((ROWS, N), F32),
            pltpu.VMEM((2, ROWS, N), BF16),
            pltpu.VMEM((3, R, N), F32),
            pltpu.VMEM((2, R, N), F32),
            pltpu.VMEM((R, N), F32),
            pltpu.VMEM((R, 2 * R), F32),
            pltpu.VMEM((R, R), F32),
            pltpu.VMEM((R, R), F32),
            pltpu.VMEM((3, 3, 64, N), F32),
            pltpu.VMEM((3, 64, N), F32),
            pltpu.VMEM((3, 3, 16, N), F32),
            pltpu.VMEM((3, 4, 16, N), F32),
            pltpu.VMEM((4, 2, 64, N // 4), F32),
            pltpu.VMEM((4, 2, 64, N // 4), F32),
            pltpu.VMEM((4, 2, 64, N // 2), F32),
            pltpu.VMEM((4, 64, N // 2), F32),
            pltpu.VMEM((4, 3, 16, N // 2), F32),
            pltpu.VMEM((2, R, N), F32),
            pltpu.VMEM((2, R, R), F32),
            pltpu.VMEM((3, 64, R), F32),
            pltpu.VMEM((64, R), F32),
            pltpu.VMEM((3, 16, R), F32),
            pltpu.SemaphoreType.DMA((17,)),
            pltpu.SemaphoreType.DMA((COPIES,)),
            pltpu.SemaphoreType.DMA((COPIES,)),
        ],
        compiler_params=pltpu.CompilerParams(
            collective_id=0, has_side_effects=True, vmem_limit_bytes=60 * 1024 * 1024
        ),
    )(grads, error, proj_old)
    inputs = (wide, mixer, local, grads, error, cross, summed, moment1, moment2)
    outputs = (
        shape((2, ROWS, N), BF16),
        shape((2, ROWS, N), BF16),
        shape((2, ROWS, R), F32),
        shape((2, R, N), F32),
        shape((2, R, N), F32),
    )
    update, error_new, proj_new, first_new, second_new = pl.pallas_call(
        final_kernel,
        out_shape=outputs,
        in_specs=[anywhere] * 9,
        out_specs=(anywhere,) * 5,
        scratch_shapes=[pltpu.VMEM(one.shape, one.dtype) for one in inputs + outputs]
        + [pltpu.SemaphoreType.DMA((2, 9)), pltpu.SemaphoreType.DMA((2, 5))],
        compiler_params=pltpu.CompilerParams(vmem_limit_bytes=60 * 1024 * 1024),
    )(*inputs)
    return (update, error_new[None], proj_new, first_new, second_new)


def solution(mesh):
    in_specs = (
        P("dp", None, "fsdp", None),
        P("dp", None, "fsdp", None),
        P(None, "fsdp", None),
        P(),
        P(),
    )
    out_specs = (
        P(None, "fsdp", None),
        P("dp", None, "fsdp", None),
        P(None, "fsdp", None),
        P(),
        P(),
    )
    return jax.shard_map(
        on_device, mesh=mesh, in_specs=in_specs, out_specs=out_specs, check_vma=False
    )
```

```python
import functools
import jax
import jax.numpy as jnp
from jax import lax
from jax.experimental import pallas as pl
from jax.experimental.pallas import tpu as pltpu
from jax.sharding import PartitionSpec as P

F32 = jnp.float32
BF16 = jnp.bfloat16
MESH = pl.DeviceIdType.MESH
N = 1024
R = 256
ROWS = 512
PIECE = 128
BLOCK = 64
GROUP = 16
COPIES = 160
CUTS = 2
COLUMN_PARTS = ((0, 512, "zyx"), (512, 1024, "yzx"))
MIDDLE_PARTS = ((0, 384, "zyx"), (384, 768, "yxz"), (768, 1024, "xzy"))
LAST_PARTS = ((0, 256, "xzy"), (256, 512, "xyz"), (512, 768, "zyx"), (768, 1024, "yzx"))


def dot(a, b, ca=1, cb=0):
    return lax.dot_general(
        a,
        b,
        (((ca,), (cb,)), ((), ())),
        precision=lax.Precision.HIGHEST,
        preferred_element_type=F32,
    )


def halves(value):
    high = value.astype(BF16)
    return high, (value - high.astype(F32)).astype(BF16)


def dot_bf16(a, b, ca=1, cb=0):
    return lax.dot_general(a, b, (((ca,), (cb,)), ((), ())), preferred_element_type=F32)


def dot_halves(a, b, ca=1, cb=0):
    small = dot_bf16(a[0], b[1], ca, cb) + dot_bf16(a[1], b[0], ca, cb)
    return dot_bf16(a[0], b[0], ca, cb) + small


class Place:
    def __init__(self):
        dp, fsdp = lax.axis_index("dp"), lax.axis_index("fsdp")
        self.at = {
            "x": lax.div(dp, 2),
            "c": lax.rem(dp, 2),
            "y": lax.div(fsdp, 4),
            "z": lax.rem(fsdp, 4),
        }

    def peer(self, axis, step):
        new = dict(self.at)
        c = self.at["c"]
        if axis == "c":
            new["c"] = 1 - c
        elif axis == "a":
            new["z"] = lax.rem(new["z"] + (1 - c) * step, 4)
            new["y"] = lax.rem(new["y"] + c * step, 4)
        elif axis == "b":
            new["z"] = lax.rem(new["z"] + c * step, 4)
            new["y"] = lax.rem(new["y"] + (1 - c) * step, 4)
        else:
            new[axis] = lax.rem(new[axis] + step, 4)
        return (new["x"] * 2 + new["c"], new["y"] * 4 + new["z"])

    def index(self, axis):
        c, y, z = self.at["c"], self.at["y"], self.at["z"]
        if axis == "a":
            return z * (1 - c) + y * c
        if axis == "b":
            return y * (1 - c) + z * c
        return self.at[axis]


class Links:
    def __init__(self, place, send_sems, recv_sems):
        self.place, self.send_sems, self.recv_sems = place, send_sems, recv_sems
        self.used = 0
        self.started = []

    def slot(self):
        at = self.used
        self.used += 1
        return at

    def copy(self, src, dst, axis, step, at):
        return pltpu.make_async_remote_copy(
            src_ref=src,
            dst_ref=dst,
            send_sem=self.send_sems.at[at],
            recv_sem=self.recv_sems.at[at],
            device_id=self.place.peer(axis, step),
            device_id_type=MESH,
        )

    def send(self, src, dst, axis, step):
        copy = self.copy(src, dst, axis, step, self.slot())
        copy.start()
        self.started.append(copy)
        return copy

    def drain(self):
        assert self.used <= COPIES
        for copy in self.started:
            copy.wait_send()


class Group:
    def __init__(self, links, whole):
        self.links, self.at = links, links.slot()
        self.all = links.copy(whole, whole, "c", 1, self.at)
        links.started.append(self.all)

    def send(self, src, dst, axis, step):
        self.links.copy(src, dst, axis, step, self.at).start()

    def wait(self):
        self.all.wait_recv()


def rows_of(index, size):
    return pl.ds(pl.multiple_of(index * size, size), size)


class Reduce:
    def __init__(self, links, src, out, base, rows, lanes, axes, scratch):
        self.links, self.src, self.out, self.lanes, self.axes = links, src, out, lanes, axes
        self.base, self.large, self.small = base, rows // 4, rows // 16
        self.first, self.mine, self.second, self.last = scratch
        self.group = None

    def large_rows(self, index):
        return pl.ds(pl.multiple_of(self.base + index * self.large, 8), self.large)

    def small_rows(self, index):
        return pl.ds(pl.multiple_of(index * self.small, 8), self.small)

    def start(self):
        axis = self.axes[0]
        me = self.links.place.index(axis)
        self.group = Group(self.links, self.first)
        for step in (2, 1, 3):
            block = self.large_rows(lax.rem(me + step, 4))
            self.group.send(self.src.at[block, self.lanes], self.first.at[step - 1], axis, step)

    def wait(self):
        self.group.wait()

    def second_stage(self):
        self.wait()
        place = self.links.place
        total = self.src[self.large_rows(place.index(self.axes[0])), self.lanes]
        for slot in range(3):
            total = total + self.first[slot]
        self.mine[...] = total
        axis = self.axes[1]
        me = place.index(axis)
        self.group = Group(self.links, self.second)
        for step in (2, 1, 3):
            block = self.small_rows(lax.rem(me + step, 4))
            self.group.send(self.mine.at[block], self.second.at[step - 1], axis, step)

    def own_rows(self):
        place = self.links.place
        start = place.index(self.axes[0]) * self.large + place.index(self.axes[1]) * self.small
        return pl.ds(pl.multiple_of(self.base + start, 8), self.small)

    def third_stage(self):
        self.wait()
        place = self.links.place
        total = self.mine[self.small_rows(place.index(self.axes[1]))]
        for slot in range(3):
            total = total + self.second[slot]
        if len(self.axes) == 2:
            self.out[self.own_rows(), self.lanes] = total
            return
        axis = self.axes[2]
        me = place.index(axis)
        self.last[me] = total
        self.group = Group(self.links, self.last.at[pl.ds(0, 3)])
        for step in (2, 1, 3):
            self.group.send(self.last.at[me], self.last.at[me], axis, step)

    def gather_second(self):
        if len(self.axes) == 3:
            self.wait()
            self.out[self.own_rows(), self.lanes] = (
                (self.last[0] + self.last[1]) + (self.last[2] + self.last[3])
            )
        own = self.out.at[self.own_rows(), self.lanes]
        self.group = Group(self.links, self.second)
        for step in (2, 1, 3):
            self.group.send(own, own, self.axes[1], step)

    def gather_first(self):
        self.wait()
        axis = self.axes[0]
        own = self.out.at[self.large_rows(self.links.place.index(axis)), self.lanes]
        self.group = Group(self.links, self.first)
        for step in (2, 1, 3):
            self.group.send(own, own, axis, step)


class Ring:
    def __init__(self, links, axis, src, size, low, width, scratch):
        self.links, self.axis, self.src, self.size = links, axis, src, size
        self.via, self.sums, self.got = scratch
        self.half = half = width // 2
        self.lanes = pl.ds(low, width)
        self.left, self.right = pl.ds(low, half), pl.ds(low + half, half)

    def block(self, step):
        return rows_of(lax.rem(self.links.place.index(self.axis) + step, 4), self.size)

    def scatter_far(self):
        far = self.block(2)
        self.far = (
            self.links.send(self.src.at[far, self.left], self.via.at[0], self.axis, 1),
            self.links.send(self.src.at[far, self.right], self.via.at[1], self.axis, 3),
        )
        self.groups = Group(self.links, self.got.at[0]), Group(self.links, self.got.at[1])

    def scatter_next(self):
        target = self.got.at[0, :, pl.ds(self.half, self.half)]
        self.groups[0].send(self.src.at[self.block(1), self.right], target, self.axis, 1)

    def scatter_back(self):
        target = self.got.at[1, :, pl.ds(0, self.half)]
        self.groups[1].send(self.src.at[self.block(3), self.left], target, self.axis, 3)

    def relay(self):
        self.far[0].wait_recv()
        self.sums[0] = self.src[self.block(1), self.left] + self.via[0]
        target = self.got.at[0, :, pl.ds(0, self.half)]
        self.groups[0].send(self.sums.at[0], target, self.axis, 1)
        self.far[1].wait_recv()
        self.sums[1] = self.src[self.block(3), self.right] + self.via[1]
        target = self.got.at[1, :, pl.ds(self.half, self.half)]
        self.groups[1].send(self.sums.at[1], target, self.axis, 3)

    def collect(self):
        self.groups[0].wait()
        self.groups[1].wait()
        return (self.src[self.block(0), self.lanes] + self.got[0]) + self.got[1]

    def gather(self, out):
        own = out.at[self.block(0), self.lanes]
        self.copies = [self.links.send(own, own, self.axis, step) for step in (1, 3)]

    def forward(self, out):
        self.group = Group(self.links, self.got.at[0])
        self.copies[0].wait_recv()
        part = out.at[self.block(3), self.left]
        self.group.send(part, part, self.axis, 1)
        self.copies[1].wait_recv()
        part = out.at[self.block(1), self.right]
        self.group.send(part, part, self.axis, 3)

    def finish(self):
        self.group.wait()


class Chunk:
    def __init__(self, links, axes, src, out, low, width, scratch):
        self.links, self.axes, self.out = links, axes, out
        self.mine, self.second = scratch[3:]
        self.ring = Ring(links, axes[0], src, 64, low, width, scratch[:3])
        self.lanes = pl.ds(low, width)

    def start(self):
        self.ring.scatter_far()
        self.ring.scatter_next()
        self.ring.scatter_back()

    def relay(self):
        self.ring.relay()

    def collect(self):
        self.mine[...] = self.ring.collect()
        axis = self.axes[1]
        me = self.links.place.index(axis)
        self.group = Group(self.links, self.second)
        for step in (2, 1, 3):
            block = rows_of(lax.rem(me + step, 4), 16)
            self.group.send(self.mine.at[block], self.second.at[step - 1], axis, step)

    def spread(self):
        self.group.wait()
        place = self.links.place
        me = place.index(self.axes[1])
        rows = pl.ds(pl.multiple_of(place.index(self.axes[0]) * 64 + me * 16, 16), 16)
        total = self.mine[rows_of(me, 16)]
        for slot in range(3):
            total = total + self.second[slot]
        self.out[rows, self.lanes] = total
        own = self.out.at[rows, self.lanes]
        self.group = Group(self.links, self.second)
        for step in (2, 1, 3):
            self.group.send(own, own, self.axes[1], step)

    def gather(self):
        self.group.wait()
        self.ring.gather(self.out)

    def forward(self):
        self.ring.forward(self.out)

    def finish(self):
        self.ring.finish()


def stages(parts):
    for part in parts:
        part.second_stage()
    yield
    for part in parts:
        part.third_stage()
    yield
    for part in parts:
        part.gather_second()
    yield
    for part in parts:
        part.gather_first()
    yield
    for part in parts:
        part.wait()
    yield


def advance(steps, count):
    for _ in range(count):
        next(steps)


def eliminate(diag):
    lanes = lax.broadcasted_iota(jnp.int32, (8, 2 * BLOCK), 1)
    subs = lax.broadcasted_iota(jnp.int32, (8, 2 * BLOCK), 0)
    full = lambda value: jnp.broadcast_to(value, (8, 2 * BLOCK))
    count = BLOCK // 8
    state, pivots = [], []
    for v in range(count):
        block = jnp.concatenate([diag[8 * v : 8 * v + 8], jnp.zeros((8, BLOCK), F32)], axis=1)
        state.append(jnp.where(lanes == subs + (BLOCK + 8 * v), 1.0, block))
        pivots.append(None)
    for group in range(0, BLOCK, GROUP):
        columns = [
            [full(state[v][:, at : at + 1]) if v >= group // 8 else None for v in range(count)]
            for at in range(group, group + GROUP)
        ]
        for k in range(GROUP):
            here, sub = divmod(group + k, 8)
            pivot = full(columns[k][here][sub : sub + 1])
            inverse = 1.0 / pivot
            pivots[here] = pivot if sub == 0 else jnp.where(subs == sub, pivot, pivots[here])
            row = full(state[here][sub : sub + 1])
            heads = [full(columns[j][here][sub : sub + 1]) for j in range(k + 1, GROUP)]
            for v in range(here, count):
                factor = columns[k][v] * inverse
                if v == here:
                    factor = jnp.where(subs > sub, factor, 0.0)
                for j, head in zip(range(k + 1, GROUP), heads):
                    columns[j][v] = columns[j][v] - factor * head
                state[v] = state[v] - factor * row
    scaled = [state[v] * lax.rsqrt(pivots[v]) for v in range(count)]
    return jnp.concatenate(scaled, axis=0)[:, BLOCK:]


def factor_steps(work):
    rows = lax.broadcasted_iota(jnp.int32, (R, R), 0)
    lanes = lax.broadcasted_iota(jnp.int32, (R, R), 1)
    work[:, R:] = (rows == lanes).astype(F32)
    for block in range(R // BLOCK):
        low, high = block * BLOCK, (block + 1) * BLOCK
        scale = eliminate(work[low:high, low:high])
        yield
        strip = dot(scale, work[low:high, :])
        work[low:high, :] = strip
        if high < R:
            work[high:, :] = work[high:, :] - dot(strip[:, high:R], strip, 0, 0)
        yield


def main_kernel(
    grads_any, error_any, proj_any, wide, local, summed, mixer, cross, grads, error, proj_old,
    turned, a_send, a_recv, pair, s_via, s_sums, s_got, total, total_parts, bufs, outs, normal,
    work, gram, unmixed, first, mine, second, last, uvia, usums, ugot, umine, usecond, ubuf,
    grams, gfirst, gmine, gsecond, in_sems, send_sems, recv_sems,
):
    place = Place()
    links = Links(place, send_sems, recv_sems)
    c, x = place.at["c"], place.at["x"]
    other = 1 - c
    order = (2, 1, 3, 0)
    blocks = [rows_of(lax.rem(x + step, 4), PIECE) for step in order]

    loads = []

    def load(source, target):
        copy = pltpu.make_async_copy(source, target, in_sems.at[len(loads)])
        copy.start()
        loads.append(copy)
        return copy

    def load_rows(matrix, rows):
        return [
            load(source.at[matrix, rows], target.at[matrix, rows])
            for source, target in ((grads_any, grads), (error_any, error))
        ]

    barrier = pltpu.get_barrier_semaphore()
    partners = [("c", 1)] + [(axis, step) for axis in "xyz" for step in (1, 2, 3)]
    for axis, step in partners:
        pl.semaphore_signal(barrier, inc=1, device_id=place.peer(axis, step), device_id_type=MESH)
    sent_loads = [load_rows(other, rows) for rows in blocks]
    proj_load = load(proj_any.at[c], proj_old)
    kept_loads = [load_rows(c, rows) for rows in blocks]

    for rows, copies in zip(blocks, sent_loads):
        for copy in copies:
            copy.wait()
        a_send[rows, :] = grads[other, rows, :].astype(F32) + error[other, rows, :].astype(F32)
    pl.semaphore_wait(barrier, len(partners))
    core_copies = [links.send(a_send.at[rows], a_recv.at[rows], "c", 1) for rows in blocks]
    proj_load.wait()
    turned[0], turned[1] = halves(proj_old[...].T)
    for rows, copies in zip(blocks, kept_loads):
        for copy in copies:
            copy.wait()
        pair[rows, :] = grads[c, rows, :].astype(F32) + error[c, rows, :].astype(F32)

    replicas = Ring(links, "x", pair, PIECE, 0, N, (s_via, s_sums, s_got))
    sends = (replicas.scatter_far, replicas.scatter_next, replicas.scatter_back, lambda: None)
    for at, (send, rows, copy) in enumerate(zip(sends, blocks, core_copies)):
        copy.wait_recv()
        pair[rows, :] = pair[rows, :] + a_recv[rows, :]
        send()
        left = (turned[0, :, rows], turned[1, :, rows])
        for low in range(0, N, 256):
            lanes = pl.ds(low, 256)
            piece = dot_halves(left, halves(pair[rows, lanes]))
            bufs[0, :, lanes] = piece if at == 0 else bufs[0, :, lanes] + piece

    def reducers(at, src, out, parts, cuts):
        made = []
        rows = R // cuts
        for cut in range(cuts):
            large, small = pl.ds(cut * rows // 4, rows // 4), pl.ds(cut * rows // 16, rows // 16)
            for low, high, axes in parts:
                lanes = pl.ds(low, high - low)
                scratch = (
                    first.at[at, :, large, lanes],
                    mine.at[at, large, lanes],
                    second.at[at, :, small, lanes],
                    last.at[at, :, small, lanes],
                )
                made.append(Reduce(links, src, out, cut * rows, rows, lanes, axes, scratch))
        return made

    parts = reducers(0, bufs.at[0], outs.at[0], COLUMN_PARTS, CUTS)
    for part in parts:
        part.start()
    steps = stages(parts)
    replicas.relay()
    advance(steps, 2)
    own_total = replicas.collect()
    total[rows_of(x, PIECE), :] = own_total
    replicas.gather(total)
    total_parts[0, rows_of(x, PIECE)], total_parts[1, rows_of(x, PIECE)] = halves(own_total)
    advance(steps, 3)
    def spread(at, wide_part, out, axes, cuts):
        made = reducers(at, bufs.at[at], out, axes, cuts)
        left = halves(wide_part)
        own = rows_of(x, PIECE)
        for low, high, _ in axes:
            lanes = pl.ds(low, high - low)
            bufs[at, :, lanes] = dot_halves(
                left, (total_parts[0, own, lanes], total_parts[1, own, lanes])
            )
        for part in made:
            part.start()
        return stages(made)

    def widen(columns, rows):
        return dot_halves(
            halves(columns), (total_parts[0, rows], total_parts[1, rows]), 1, 1
        )

    steps = spread(1, widen(outs[0], rows_of(x, PIECE)), outs.at[1], MIDDLE_PARTS, CUTS)
    replicas.forward(total)
    for step in (1, 3):
        rows = replicas.block(step)
        total_parts[0, rows], total_parts[1, rows] = halves(total[rows])
    advance(steps, 4)
    replicas.finish()
    rows = replicas.block(2)
    total_parts[0, rows], total_parts[1, rows] = halves(total[rows])
    next(steps)
    size = jnp.sum(outs[0] * outs[1], axis=1, keepdims=True)
    scale = 1.0 / jnp.sqrt(size)
    normal[...] = outs[1] * scale
    wide[c] = widen(normal[...], pl.ds(0, ROWS))
    wide_copy = links.send(wide.at[c], wide.at[c], "c", 1)
    grams[0] = dot(wide[c], wide[c], 1, 1)
    gram_parts = []
    for low, axes in ((0, "zy"), (128, "yz")):
        lanes = pl.ds(low, 128)
        scratch = (gfirst.at[:, :, lanes], gmine.at[:, lanes], gsecond.at[:, :, lanes], None)
        gram_parts.append(Reduce(links, grams.at[0], grams.at[1], 0, R, lanes, axes, scratch))
    for part in gram_parts:
        part.start()
    g_steps = stages(gram_parts)
    z_steps = spread(2, wide[c, :, rows_of(x, PIECE)], summed.at[c], LAST_PARTS, 1)

    chunks = []
    width = N // 2

    def launch(matrix):
        high, small = halves(wide[matrix])
        for half, axes in ((0, "ab"), (1, "ba")):
            for low in range(half * width, (half + 1) * width, 256):
                lanes = pl.ds(low, 256)
                g, e = grads[matrix, :, lanes], error[matrix, :, lanes]
                rest = dot_bf16(small, g) + dot_bf16(small, e)
                ubuf[matrix, :, lanes] = (dot_bf16(high, g) + dot_bf16(high, e)) + rest
            at = len(chunks)
            scratch = (uvia.at[at], usums.at[at], ugot.at[at], umine.at[at], usecond.at[at])
            chunks.append(
                Chunk(
                    links, axes, ubuf.at[matrix], local.at[matrix], half * width, width, scratch
                )
            )
            chunks[-1].start()

    launch(c)
    work[:, :R] = dot(outs[0] * scale, normal[...], 1, 1)
    wide_copy.wait_recv()
    next(g_steps)
    launch(other)
    early, late = chunks[:2], chunks[2:]
    factor = factor_steps(work)
    advance(factor, 1)
    advance(g_steps, 2)
    for chunk in early:
        chunk.relay()
    advance(factor, 1)
    next(z_steps)
    for chunk in late:
        chunk.relay()
    advance(factor, 1)
    next(g_steps)
    for chunk in early:
        chunk.collect()
    advance(factor, 1)
    next(z_steps)
    for chunk in late:
        chunk.collect()
    advance(factor, 2)
    for chunk in early:
        chunk.spread()
    next(z_steps)
    advance(factor, 2)
    unmixed[...] = work[:, R:]
    for chunk in late:
        chunk.spread()
    next(g_steps)
    work[:, :R] = dot(dot(unmixed[...], grams[1]), unmixed[...], 1, 1)
    next(z_steps)
    factor = factor_steps(work)
    advance(factor, 1)
    for chunk in early:
        chunk.gather()
    advance(factor, 1)
    for chunk in late:
        chunk.gather()
    advance(factor, 2)
    next(z_steps)
    z_copy = links.send(summed.at[c], summed.at[c], "c", 1)
    for chunk in early:
        chunk.forward()
    gram[...] = dot(normal[...], outs[0], 1, 1)
    advance(factor, 2)
    for chunk in late:
        chunk.forward()
    advance(factor, 2)
    mixer[c] = dot(work[:, R:], unmixed[...])
    m_copy = links.send(mixer.at[c], mixer.at[c], "c", 1)
    cross[c] = dot(mixer[c], gram[...])
    r_copy = links.send(cross.at[c], cross.at[c], "c", 1)
    for chunk in chunks:
        chunk.finish()
    z_copy.wait_recv()
    m_copy.wait_recv()
    r_copy.wait_recv()
    links.drain()


def final_kernel(
    wide, mixer, local, grads, error, cross, summed, moment1, moment2,
    update, error_new, proj_new, first_new, second_new,
    v_wide, v_mixer, v_local, v_grads, v_error, v_cross, v_summed, v_moment1, v_moment2,
    v_update, v_error_new, v_proj_new, v_first_new, v_second_new, in_sems, out_sems,
):
    sources = (wide, mixer, local, grads, error, cross, summed, moment1, moment2)
    holds = (v_wide, v_mixer, v_local, v_grads, v_error, v_cross, v_summed, v_moment1, v_moment2)
    loads = []
    for k in range(2):
        made = [
            pltpu.make_async_copy(source.at[k], hold.at[k], in_sems.at[k, at])
            for at, (source, hold) in enumerate(zip(sources, holds))
        ]
        for copy in made:
            copy.start()
        loads.append(made)
    stores = []

    def store(hold, result, k, at):
        copy = pltpu.make_async_copy(hold.at[k], result.at[k], out_sems.at[k, at])
        copy.start()
        stores.append(copy)

    for k in range(2):
        loads[k][0].wait()
        loads[k][1].wait()
        mix = v_mixer[k]
        basis = dot(v_wide[k], mix, 0, 1)
        v_proj_new[k] = basis
        store(v_proj_new, proj_new, k, 2)
        basis, mix = halves(basis), halves(mix)
        for at in range(2, 9):
            loads[k][at].wait()
        rotation = v_cross[k]
        turn, spin = halves(rotation), halves(rotation * rotation)
        for at in range(0, N, 256):
            lanes = pl.ds(at, 256)
            projected = dot_halves(mix, halves(v_local[k, :, lanes]))
            back = dot_halves(basis, halves(projected))
            accrued = v_grads[k, :, lanes].astype(F32) + v_error[k, :, lanes].astype(F32)
            v_error_new[k, :, lanes] = (accrued - back).astype(BF16)
            grad_proj = dot_halves(mix, halves(v_summed[k, :, lanes])) / 8.0
            m1, m2 = v_moment1[k, :, lanes], v_moment2[k, :, lanes]
            turned = dot_halves(turn, halves(m1))
            spun = dot_halves(spin, halves(jnp.abs(m2 - m1 * m1)))
            one = 0.9 * turned + 0.1 * grad_proj
            two = 0.99 * (spun + turned * turned) + 0.01 * grad_proj * grad_proj
            v_first_new[k, :, lanes] = one
            v_second_new[k, :, lanes] = two
            step = one / (jnp.sqrt(two) + 1e-06)
            v_update[k, :, lanes] = dot_halves(basis, halves(step)).astype(BF16)
        store(v_error_new, error_new, k, 1)
        store(v_first_new, first_new, k, 3)
        store(v_second_new, second_new, k, 4)
        store(v_update, update, k, 0)
    for copy in stores:
        copy.wait()


def on_device(grads, error, proj_old, moment1, moment2):
    grads, error = grads[0], error[0]
    vmem = pl.BlockSpec(memory_space=pltpu.VMEM)
    anywhere = pl.BlockSpec(memory_space=pl.ANY)
    shape = jax.ShapeDtypeStruct
    wide, local, summed, mixer, cross = pl.pallas_call(
        main_kernel,
        out_shape=(
            shape((2, R, ROWS), F32),
            shape((2, R, N), F32),
            shape((2, R, N), F32),
            shape((2, R, R), F32),
            shape((2, R, R), F32),
        ),
        in_specs=[anywhere] * 3,
        out_specs=(vmem,) * 5,
        scratch_shapes=[
            pltpu.VMEM((2, ROWS, N), BF16),
            pltpu.VMEM((2, ROWS, N), BF16),
            pltpu.VMEM((ROWS, R), F32),
            pltpu.VMEM((2, R, ROWS), BF16),
            pltpu.VMEM((ROWS, N), F32),
            pltpu.VMEM((ROWS, N), F32),
            pltpu.VMEM((ROWS, N), F32),
            pltpu.VMEM((2, PIECE, N // 2), F32),
            pltpu.VMEM((2, PIECE, N // 2), F32),
            pltpu.VMEM((2, PIECE, N), F32),
            pltpu.VMEM((ROWS, N), F32),
            pltpu.VMEM((2, ROWS, N), BF16),
            pltpu.VMEM((3, R, N), F32),
            pltpu.VMEM((2, R, N), F32),
            pltpu.VMEM((R, N), F32),
            pltpu.VMEM((R, 2 * R), F32),
            pltpu.VMEM((R, R), F32),
            pltpu.VMEM((R, R), F32),
            pltpu.VMEM((3, 3, 64, N), F32),
            pltpu.VMEM((3, 64, N), F32),
            pltpu.VMEM((3, 3, 16, N), F32),
            pltpu.VMEM((3, 4, 16, N), F32),
            pltpu.VMEM((4, 2, 64, N // 4), F32),
            pltpu.VMEM((4, 2, 64, N // 4), F32),
            pltpu.VMEM((4, 2, 64, N // 2), F32),
            pltpu.VMEM((4, 64, N // 2), F32),
            pltpu.VMEM((4, 3, 16, N // 2), F32),
            pltpu.VMEM((2, R, N), F32),
            pltpu.VMEM((2, R, R), F32),
            pltpu.VMEM((3, 64, R), F32),
            pltpu.VMEM((64, R), F32),
            pltpu.VMEM((3, 16, R), F32),
            pltpu.SemaphoreType.DMA((17,)),
            pltpu.SemaphoreType.DMA((COPIES,)),
            pltpu.SemaphoreType.DMA((COPIES,)),
        ],
        compiler_params=pltpu.CompilerParams(
            collective_id=0, has_side_effects=True, vmem_limit_bytes=60 * 1024 * 1024
        ),
    )(grads, error, proj_old)
    inputs = (wide, mixer, local, grads, error, cross, summed, moment1, moment2)
    outputs = (
        shape((2, ROWS, N), BF16),
        shape((2, ROWS, N), BF16),
        shape((2, ROWS, R), F32),
        shape((2, R, N), F32),
        shape((2, R, N), F32),
    )
    update, error_new, proj_new, first_new, second_new = pl.pallas_call(
        final_kernel,
        out_shape=outputs,
        in_specs=[anywhere] * 9,
        out_specs=(anywhere,) * 5,
        scratch_shapes=[pltpu.VMEM(one.shape, one.dtype) for one in inputs + outputs]
        + [pltpu.SemaphoreType.DMA((2, 9)), pltpu.SemaphoreType.DMA((2, 5))],
        compiler_params=pltpu.CompilerParams(vmem_limit_bytes=60 * 1024 * 1024),
    )(*inputs)
    return (update, error_new[None], proj_new, first_new, second_new)


def solution(mesh):
    in_specs = (
        P("dp", None, "fsdp", None),
        P("dp", None, "fsdp", None),
        P(None, "fsdp", None),
        P(),
        P(),
    )
    out_specs = (
        P(None, "fsdp", None),
        P("dp", None, "fsdp", None),
        P(None, "fsdp", None),
        P(),
        P(),
    )
    return jax.shard_map(
        on_device, mesh=mesh, in_specs=in_specs, out_specs=out_specs, check_vma=False
    )
```

```python
import functools
import jax
import jax.numpy as jnp
from jax import lax
from jax.experimental import pallas as pl
from jax.experimental.pallas import tpu as pltpu
from jax.sharding import PartitionSpec as P

F32 = jnp.float32
BF16 = jnp.bfloat16
MESH = pl.DeviceIdType.MESH
N = 1024
R = 256
ROWS = 512
PIECE = 128
BLOCK = 64
GROUP = 16
COPIES = 160
CUTS = 2
LANES = 512
COLUMN_PARTS = ((0, 512, "zyx"), (512, 1024, "yzx"))
MIDDLE_PARTS = ((0, 384, "zyx"), (384, 768, "yxz"), (768, 1024, "xzy"))
LAST_PARTS = ((0, 256, "xzy"), (256, 512, "xyz"), (512, 768, "zyx"), (768, 1024, "yzx"))


def dot(a, b, ca=1, cb=0):
    return lax.dot_general(
        a,
        b,
        (((ca,), (cb,)), ((), ())),
        precision=lax.Precision.HIGHEST,
        preferred_element_type=F32,
    )


def halves(value):
    high = value.astype(BF16)
    return high, (value - high.astype(F32)).astype(BF16)


def dot_bf16(a, b, ca=1, cb=0):
    return lax.dot_general(a, b, (((ca,), (cb,)), ((), ())), preferred_element_type=F32)


def dot_halves(a, b, ca=1, cb=0):
    small = dot_bf16(a[0], b[1], ca, cb) + dot_bf16(a[1], b[0], ca, cb)
    return dot_bf16(a[0], b[0], ca, cb) + small


class Place:
    def __init__(self):
        dp, fsdp = lax.axis_index("dp"), lax.axis_index("fsdp")
        self.at = {
            "x": lax.div(dp, 2),
            "c": lax.rem(dp, 2),
            "y": lax.div(fsdp, 4),
            "z": lax.rem(fsdp, 4),
        }

    def peer(self, axis, step):
        new = dict(self.at)
        c = self.at["c"]
        if axis == "c":
            new["c"] = 1 - c
        elif axis == "a":
            new["z"] = lax.rem(new["z"] + (1 - c) * step, 4)
            new["y"] = lax.rem(new["y"] + c * step, 4)
        elif axis == "b":
            new["z"] = lax.rem(new["z"] + c * step, 4)
            new["y"] = lax.rem(new["y"] + (1 - c) * step, 4)
        else:
            new[axis] = lax.rem(new[axis] + step, 4)
        return (new["x"] * 2 + new["c"], new["y"] * 4 + new["z"])

    def index(self, axis):
        c, y, z = self.at["c"], self.at["y"], self.at["z"]
        if axis == "a":
            return z * (1 - c) + y * c
        if axis == "b":
            return y * (1 - c) + z * c
        return self.at[axis]


class Links:
    def __init__(self, place, send_sems, recv_sems):
        self.place, self.send_sems, self.recv_sems = place, send_sems, recv_sems
        self.used = 0
        self.started = []

    def slot(self):
        at = self.used
        self.used += 1
        return at

    def copy(self, src, dst, axis, step, at):
        return pltpu.make_async_remote_copy(
            src_ref=src,
            dst_ref=dst,
            send_sem=self.send_sems.at[at],
            recv_sem=self.recv_sems.at[at],
            device_id=self.place.peer(axis, step),
            device_id_type=MESH,
        )

    def send(self, src, dst, axis, step):
        copy = self.copy(src, dst, axis, step, self.slot())
        copy.start()
        self.started.append(copy)
        return copy

    def drain(self):
        assert self.used <= COPIES
        for copy in self.started:
            copy.wait_send()


class Group:
    def __init__(self, links, whole):
        self.links, self.at = links, links.slot()
        self.all = links.copy(whole, whole, "c", 1, self.at)
        links.started.append(self.all)

    def send(self, src, dst, axis, step):
        self.links.copy(src, dst, axis, step, self.at).start()

    def wait(self):
        self.all.wait_recv()


def rows_of(index, size):
    return pl.ds(pl.multiple_of(index * size, size), size)


class Reduce:
    def __init__(self, links, src, out, base, rows, lanes, axes, scratch):
        self.links, self.src, self.out, self.lanes, self.axes = links, src, out, lanes, axes
        self.base, self.large, self.small = base, rows // 4, rows // 16
        self.first, self.mine, self.second, self.last = scratch
        self.group = None

    def large_rows(self, index):
        return pl.ds(pl.multiple_of(self.base + index * self.large, 8), self.large)

    def small_rows(self, index):
        return pl.ds(pl.multiple_of(index * self.small, 8), self.small)

    def start(self):
        axis = self.axes[0]
        me = self.links.place.index(axis)
        self.group = Group(self.links, self.first)
        for step in (2, 1, 3):
            block = self.large_rows(lax.rem(me + step, 4))
            self.group.send(self.src.at[block, self.lanes], self.first.at[step - 1], axis, step)

    def wait(self):
        self.group.wait()

    def second_stage(self):
        self.wait()
        place = self.links.place
        total = self.src[self.large_rows(place.index(self.axes[0])), self.lanes]
        for slot in range(3):
            total = total + self.first[slot]
        self.mine[...] = total
        axis = self.axes[1]
        me = place.index(axis)
        self.group = Group(self.links, self.second)
        for step in (2, 1, 3):
            block = self.small_rows(lax.rem(me + step, 4))
            self.group.send(self.mine.at[block], self.second.at[step - 1], axis, step)

    def own_rows(self):
        place = self.links.place
        start = place.index(self.axes[0]) * self.large + place.index(self.axes[1]) * self.small
        return pl.ds(pl.multiple_of(self.base + start, 8), self.small)

    def third_stage(self):
        self.wait()
        place = self.links.place
        total = self.mine[self.small_rows(place.index(self.axes[1]))]
        for slot in range(3):
            total = total + self.second[slot]
        if len(self.axes) == 2:
            self.out[self.own_rows(), self.lanes] = total
            return
        axis = self.axes[2]
        me = place.index(axis)
        self.last[me] = total
        self.group = Group(self.links, self.last.at[pl.ds(0, 3)])
        for step in (2, 1, 3):
            self.group.send(self.last.at[me], self.last.at[me], axis, step)

    def gather_second(self):
        if len(self.axes) == 3:
            self.wait()
            self.out[self.own_rows(), self.lanes] = (
                (self.last[0] + self.last[1]) + (self.last[2] + self.last[3])
            )
        own = self.out.at[self.own_rows(), self.lanes]
        self.group = Group(self.links, self.second)
        for step in (2, 1, 3):
            self.group.send(own, own, self.axes[1], step)

    def gather_first(self):
        self.wait()
        axis = self.axes[0]
        own = self.out.at[self.large_rows(self.links.place.index(axis)), self.lanes]
        self.group = Group(self.links, self.first)
        for step in (2, 1, 3):
            self.group.send(own, own, axis, step)


class Ring:
    def __init__(self, links, axis, src, size, low, width, scratch):
        self.links, self.axis, self.src, self.size = links, axis, src, size
        self.via, self.sums, self.got = scratch
        self.half = half = width // 2
        self.lanes = pl.ds(low, width)
        self.left, self.right = pl.ds(low, half), pl.ds(low + half, half)

    def block(self, step):
        return rows_of(lax.rem(self.links.place.index(self.axis) + step, 4), self.size)

    def scatter_far(self):
        far = self.block(2)
        self.far = (
            self.links.send(self.src.at[far, self.left], self.via.at[0], self.axis, 1),
            self.links.send(self.src.at[far, self.right], self.via.at[1], self.axis, 3),
        )
        self.groups = Group(self.links, self.got.at[0]), Group(self.links, self.got.at[1])

    def scatter_next(self):
        target = self.got.at[0, :, pl.ds(self.half, self.half)]
        self.groups[0].send(self.src.at[self.block(1), self.right], target, self.axis, 1)

    def scatter_back(self):
        target = self.got.at[1, :, pl.ds(0, self.half)]
        self.groups[1].send(self.src.at[self.block(3), self.left], target, self.axis, 3)

    def relay(self):
        self.far[0].wait_recv()
        self.sums[0] = self.src[self.block(1), self.left] + self.via[0]
        target = self.got.at[0, :, pl.ds(0, self.half)]
        self.groups[0].send(self.sums.at[0], target, self.axis, 1)
        self.far[1].wait_recv()
        self.sums[1] = self.src[self.block(3), self.right] + self.via[1]
        target = self.got.at[1, :, pl.ds(self.half, self.half)]
        self.groups[1].send(self.sums.at[1], target, self.axis, 3)

    def collect(self):
        self.groups[0].wait()
        self.groups[1].wait()
        return (self.src[self.block(0), self.lanes] + self.got[0]) + self.got[1]

    def gather(self, out):
        own = out.at[self.block(0), self.lanes]
        self.copies = [self.links.send(own, own, self.axis, step) for step in (1, 3)]

    def forward(self, out):
        self.group = Group(self.links, self.got.at[0])
        self.copies[0].wait_recv()
        part = out.at[self.block(3), self.left]
        self.group.send(part, part, self.axis, 1)
        self.copies[1].wait_recv()
        part = out.at[self.block(1), self.right]
        self.group.send(part, part, self.axis, 3)

    def finish(self):
        self.group.wait()


class Chunk:
    def __init__(self, links, axes, src, out, low, width, scratch):
        self.links, self.axes, self.out = links, axes, out
        self.mine, self.second = scratch[3:]
        self.ring = Ring(links, axes[0], src, 64, low, width, scratch[:3])
        self.lanes = pl.ds(low, width)

    def start(self):
        self.ring.scatter_far()
        self.ring.scatter_next()
        self.ring.scatter_back()

    def relay(self):
        self.ring.relay()

    def collect(self):
        self.mine[...] = self.ring.collect()
        axis = self.axes[1]
        me = self.links.place.index(axis)
        self.group = Group(self.links, self.second)
        for step in (2, 1, 3):
            block = rows_of(lax.rem(me + step, 4), 16)
            self.group.send(self.mine.at[block], self.second.at[step - 1], axis, step)

    def spread(self):
        self.group.wait()
        place = self.links.place
        me = place.index(self.axes[1])
        rows = pl.ds(pl.multiple_of(place.index(self.axes[0]) * 64 + me * 16, 16), 16)
        total = self.mine[rows_of(me, 16)]
        for slot in range(3):
            total = total + self.second[slot]
        self.out[rows, self.lanes] = total
        own = self.out.at[rows, self.lanes]
        self.group = Group(self.links, self.second)
        for step in (2, 1, 3):
            self.group.send(own, own, self.axes[1], step)

    def gather(self):
        self.group.wait()
        self.ring.gather(self.out)

    def forward(self):
        self.ring.forward(self.out)

    def finish(self):
        self.ring.finish()


def stages(parts):
    for part in parts:
        part.second_stage()
    yield
    for part in parts:
        part.third_stage()
    yield
    for part in parts:
        part.gather_second()
    yield
    for part in parts:
        part.gather_first()
    yield
    for part in parts:
        part.wait()
    yield


def advance(steps, count):
    for _ in range(count):
        next(steps)


def eliminate(diag):
    lanes = lax.broadcasted_iota(jnp.int32, (8, 2 * BLOCK), 1)
    subs = lax.broadcasted_iota(jnp.int32, (8, 2 * BLOCK), 0)
    full = lambda value: jnp.broadcast_to(value, (8, 2 * BLOCK))
    count = BLOCK // 8
    state, pivots = [], []
    for v in range(count):
        block = jnp.concatenate([diag[8 * v : 8 * v + 8], jnp.zeros((8, BLOCK), F32)], axis=1)
        state.append(jnp.where(lanes == subs + (BLOCK + 8 * v), 1.0, block))
        pivots.append(None)
    for group in range(0, BLOCK, GROUP):
        columns = [
            [full(state[v][:, at : at + 1]) if v >= group // 8 else None for v in range(count)]
            for at in range(group, group + GROUP)
        ]
        for k in range(GROUP):
            here, sub = divmod(group + k, 8)
            pivot = full(columns[k][here][sub : sub + 1])
            inverse = 1.0 / pivot
            pivots[here] = pivot if sub == 0 else jnp.where(subs == sub, pivot, pivots[here])
            row = full(state[here][sub : sub + 1])
            heads = [full(columns[j][here][sub : sub + 1]) for j in range(k + 1, GROUP)]
            for v in range(here, count):
                factor = columns[k][v] * inverse
                if v == here:
                    factor = jnp.where(subs > sub, factor, 0.0)
                for j, head in zip(range(k + 1, GROUP), heads):
                    columns[j][v] = columns[j][v] - factor * head
                state[v] = state[v] - factor * row
    scaled = [state[v] * lax.rsqrt(pivots[v]) for v in range(count)]
    return jnp.concatenate(scaled, axis=0)[:, BLOCK:]


def factor_steps(work):
    rows = lax.broadcasted_iota(jnp.int32, (R, R), 0)
    lanes = lax.broadcasted_iota(jnp.int32, (R, R), 1)
    work[:, R:] = (rows == lanes).astype(F32)
    for block in range(R // BLOCK):
        low, high = block * BLOCK, (block + 1) * BLOCK
        scale = eliminate(work[low:high, low:high])
        yield
        strip = dot(scale, work[low:high, :])
        work[low:high, :] = strip
        if high < R:
            work[high:, :] = work[high:, :] - dot(strip[:, high:R], strip, 0, 0)
        yield


def main_kernel(
    grads_any, error_any, proj_any, wide, local, summed, mixer, cross, grads, error, proj_old,
    turned, a_send, a_recv, pair, s_via, s_sums, s_got, total, total_parts, bufs, outs, normal,
    work, gram, unmixed, first, mine, second, last, uvia, usums, ugot, umine, usecond, ubuf,
    grams, gfirst, gmine, gsecond, in_sems, send_sems, recv_sems,
):
    place = Place()
    links = Links(place, send_sems, recv_sems)
    c, x = place.at["c"], place.at["x"]
    other = 1 - c
    order = (2, 1, 3, 0)
    blocks = [rows_of(lax.rem(x + step, 4), PIECE) for step in order]

    loads = []

    def load(source, target):
        copy = pltpu.make_async_copy(source, target, in_sems.at[len(loads)])
        copy.start()
        loads.append(copy)
        return copy

    def load_rows(matrix, rows):
        return [
            load(source.at[matrix, rows], target.at[matrix, rows])
            for source, target in ((grads_any, grads), (error_any, error))
        ]

    barrier = pltpu.get_barrier_semaphore()
    partners = [("c", 1)] + [(axis, step) for axis in "xyz" for step in (1, 2, 3)]
    for axis, step in partners:
        pl.semaphore_signal(barrier, inc=1, device_id=place.peer(axis, step), device_id_type=MESH)
    sent_loads = [load_rows(other, rows) for rows in blocks]
    proj_load = load(proj_any.at[c], proj_old)
    kept_loads = [load_rows(c, rows) for rows in blocks]

    for rows, copies in zip(blocks, sent_loads):
        for copy in copies:
            copy.wait()
        a_send[rows, :] = grads[other, rows, :].astype(F32) + error[other, rows, :].astype(F32)
    pl.semaphore_wait(barrier, len(partners))
    core_copies = [links.send(a_send.at[rows], a_recv.at[rows], "c", 1) for rows in blocks]
    proj_load.wait()
    turned[0], turned[1] = halves(proj_old[...].T)
    for rows, copies in zip(blocks, kept_loads):
        for copy in copies:
            copy.wait()
        pair[rows, :] = grads[c, rows, :].astype(F32) + error[c, rows, :].astype(F32)

    replicas = Ring(links, "x", pair, PIECE, 0, N, (s_via, s_sums, s_got))
    sends = (replicas.scatter_far, replicas.scatter_next, replicas.scatter_back, lambda: None)
    for at, (send, rows, copy) in enumerate(zip(sends, blocks, core_copies)):
        copy.wait_recv()
        pair[rows, :] = pair[rows, :] + a_recv[rows, :]
        send()
        left = (turned[0, :, rows], turned[1, :, rows])
        for low in range(0, N, 256):
            lanes = pl.ds(low, 256)
            piece = dot_halves(left, halves(pair[rows, lanes]))
            bufs[0, :, lanes] = piece if at == 0 else bufs[0, :, lanes] + piece

    def reducers(at, src, out, parts, cuts):
        made = []
        rows = R // cuts
        for cut in range(cuts):
            large, small = pl.ds(cut * rows // 4, rows // 4), pl.ds(cut * rows // 16, rows // 16)
            for low, high, axes in parts:
                lanes = pl.ds(low, high - low)
                scratch = (
                    first.at[at, :, large, lanes],
                    mine.at[at, large, lanes],
                    second.at[at, :, small, lanes],
                    last.at[at, :, small, lanes],
                )
                made.append(Reduce(links, src, out, cut * rows, rows, lanes, axes, scratch))
        return made

    parts = reducers(0, bufs.at[0], outs.at[0], COLUMN_PARTS, CUTS)
    for part in parts:
        part.start()
    steps = stages(parts)
    replicas.relay()
    advance(steps, 2)
    own_total = replicas.collect()
    total[rows_of(x, PIECE), :] = own_total
    replicas.gather(total)
    total_parts[0, rows_of(x, PIECE)], total_parts[1, rows_of(x, PIECE)] = halves(own_total)
    advance(steps, 3)
    def spread(at, wide_part, out, axes, cuts):
        made = reducers(at, bufs.at[at], out, axes, cuts)
        left = halves(wide_part)
        own = rows_of(x, PIECE)
        for low, high, _ in axes:
            lanes = pl.ds(low, high - low)
            bufs[at, :, lanes] = dot_halves(
                left, (total_parts[0, own, lanes], total_parts[1, own, lanes])
            )
        for part in made:
            part.start()
        return stages(made)

    def widen(columns, rows):
        return dot_halves(
            halves(columns), (total_parts[0, rows], total_parts[1, rows]), 1, 1
        )

    steps = spread(1, widen(outs[0], rows_of(x, PIECE)), outs.at[1], MIDDLE_PARTS, CUTS)
    replicas.forward(total)
    for step in (1, 3):
        rows = replicas.block(step)
        total_parts[0, rows], total_parts[1, rows] = halves(total[rows])
    advance(steps, 4)
    replicas.finish()
    rows = replicas.block(2)
    total_parts[0, rows], total_parts[1, rows] = halves(total[rows])
    next(steps)
    size = jnp.sum(outs[0] * outs[1], axis=1, keepdims=True)
    scale = 1.0 / jnp.sqrt(size)
    normal[...] = outs[1] * scale
    wide[c] = widen(normal[...], pl.ds(0, ROWS))
    wide_copy = links.send(wide.at[c], wide.at[c], "c", 1)
    grams[0] = dot(wide[c], wide[c], 1, 1)
    gram_parts = []
    for low, axes in ((0, "zy"), (128, "yz")):
        lanes = pl.ds(low, 128)
        scratch = (gfirst.at[:, :, lanes], gmine.at[:, lanes], gsecond.at[:, :, lanes], None)
        gram_parts.append(Reduce(links, grams.at[0], grams.at[1], 0, R, lanes, axes, scratch))
    for part in gram_parts:
        part.start()
    g_steps = stages(gram_parts)
    z_steps = spread(2, wide[c, :, rows_of(x, PIECE)], summed.at[c], LAST_PARTS, 1)

    chunks = []
    width = N // 2

    def launch(matrix):
        high, small = halves(wide[matrix])
        for half, axes in ((0, "ab"), (1, "ba")):
            for low in range(half * width, (half + 1) * width, 256):
                lanes = pl.ds(low, 256)
                g, e = grads[matrix, :, lanes], error[matrix, :, lanes]
                rest = dot_bf16(small, g) + dot_bf16(small, e)
                ubuf[matrix, :, lanes] = (dot_bf16(high, g) + dot_bf16(high, e)) + rest
            at = len(chunks)
            scratch = (uvia.at[at], usums.at[at], ugot.at[at], umine.at[at], usecond.at[at])
            chunks.append(
                Chunk(
                    links, axes, ubuf.at[matrix], local.at[matrix], half * width, width, scratch
                )
            )
            chunks[-1].start()

    launch(c)
    work[:, :R] = dot(outs[0] * scale, normal[...], 1, 1)
    wide_copy.wait_recv()
    next(g_steps)
    launch(other)
    early, late = chunks[:2], chunks[2:]
    factor = factor_steps(work)
    advance(factor, 1)
    advance(g_steps, 2)
    for chunk in early:
        chunk.relay()
    advance(factor, 1)
    next(z_steps)
    for chunk in late:
        chunk.relay()
    advance(factor, 1)
    next(g_steps)
    for chunk in early:
        chunk.collect()
    advance(factor, 1)
    next(z_steps)
    for chunk in late:
        chunk.collect()
    advance(factor, 2)
    for chunk in early:
        chunk.spread()
    next(z_steps)
    advance(factor, 2)
    unmixed[...] = work[:, R:]
    for chunk in late:
        chunk.spread()
    next(g_steps)
    work[:, :R] = dot(dot(unmixed[...], grams[1]), unmixed[...], 1, 1)
    next(z_steps)
    factor = factor_steps(work)
    advance(factor, 1)
    for chunk in early:
        chunk.gather()
    advance(factor, 1)
    for chunk in late:
        chunk.gather()
    advance(factor, 2)
    next(z_steps)
    z_copy = links.send(summed.at[c], summed.at[c], "c", 1)
    for chunk in early:
        chunk.forward()
    gram[...] = dot(normal[...], outs[0], 1, 1)
    advance(factor, 2)
    for chunk in late:
        chunk.forward()
    advance(factor, 2)
    mixer[c] = dot(work[:, R:], unmixed[...])
    m_copy = links.send(mixer.at[c], mixer.at[c], "c", 1)
    cross[c] = dot(mixer[c], gram[...])
    r_copy = links.send(cross.at[c], cross.at[c], "c", 1)
    for chunk in chunks:
        chunk.finish()
    z_copy.wait_recv()
    m_copy.wait_recv()
    r_copy.wait_recv()
    links.drain()


def final_kernel(
    wide, mixer, local, grads, error, cross, summed, moment1, moment2,
    update, error_new, proj_new, first_new, second_new,
    v_wide, v_mixer, v_local, v_grads, v_error, v_cross, v_summed, v_moment1, v_moment2,
    v_update, v_error_new, v_proj_new, v_first_new, v_second_new, in_sems, out_sems,
):
    count = N // LANES
    whole = ((wide, v_wide), (mixer, v_mixer), (cross, v_cross))
    parted = (
        (local, v_local),
        (grads, v_grads),
        (error, v_error),
        (summed, v_summed),
        (moment1, v_moment1),
        (moment2, v_moment2),
    )
    loads, pieces = [], []
    for k in range(2):
        made = []
        for source, hold in whole:
            made.append(
                pltpu.make_async_copy(source.at[k], hold.at[k], in_sems.at[k, len(made)])
            )
            made[-1].start()
        loads.append(made)
        pieces.append([])
        used = len(whole)
        for part in range(count):
            lanes = pl.ds(part * LANES, LANES)
            made = []
            for source, hold in parted:
                made.append(
                    pltpu.make_async_copy(
                        source.at[k, :, lanes], hold.at[k, :, lanes], in_sems.at[k, used]
                    )
                )
                made[-1].start()
                used += 1
            pieces[-1].append(made)
    stores = []

    def store(source, target):
        copy = pltpu.make_async_copy(source, target, out_sems.at[len(stores)])
        copy.start()
        stores.append(copy)

    for k in range(2):
        for copy in loads[k]:
            copy.wait()
        mix = v_mixer[k]
        basis = dot(v_wide[k], mix, 0, 1)
        v_proj_new[k] = basis
        store(v_proj_new.at[k], proj_new.at[k])
        basis, mix = halves(basis), halves(mix)
        rotation = v_cross[k]
        turn, spin = halves(rotation), halves(rotation * rotation)
        for part in range(count):
            for copy in pieces[k][part]:
                copy.wait()
            lanes = pl.ds(part * LANES, LANES)
            projected = dot_halves(mix, halves(v_local[k, :, lanes]))
            back = dot_halves(basis, halves(projected))
            accrued = v_grads[k, :, lanes].astype(F32) + v_error[k, :, lanes].astype(F32)
            v_error_new[k, :, lanes] = (accrued - back).astype(BF16)
            grad_proj = dot_halves(mix, halves(v_summed[k, :, lanes])) / 8.0
            m1, m2 = v_moment1[k, :, lanes], v_moment2[k, :, lanes]
            turned = dot_halves(turn, halves(m1))
            spun = dot_halves(spin, halves(jnp.abs(m2 - m1 * m1)))
            one = 0.9 * turned + 0.1 * grad_proj
            two = 0.99 * (spun + turned * turned) + 0.01 * grad_proj * grad_proj
            v_first_new[k, :, lanes] = one
            v_second_new[k, :, lanes] = two
            step = one / (jnp.sqrt(two) + 1e-06)
            v_update[k, :, lanes] = dot_halves(basis, halves(step)).astype(BF16)
            for hold, result in (
                (v_error_new, error_new),
                (v_first_new, first_new),
                (v_second_new, second_new),
                (v_update, update),
            ):
                store(hold.at[k, :, lanes], result.at[k, :, lanes])
    for copy in stores:
        copy.wait()


def on_device(grads, error, proj_old, moment1, moment2):
    grads, error = grads[0], error[0]
    vmem = pl.BlockSpec(memory_space=pltpu.VMEM)
    anywhere = pl.BlockSpec(memory_space=pl.ANY)
    shape = jax.ShapeDtypeStruct
    wide, local, summed, mixer, cross = pl.pallas_call(
        main_kernel,
        out_shape=(
            shape((2, R, ROWS), F32),
            shape((2, R, N), F32),
            shape((2, R, N), F32),
            shape((2, R, R), F32),
            shape((2, R, R), F32),
        ),
        in_specs=[anywhere] * 3,
        out_specs=(vmem,) * 5,
        scratch_shapes=[
            pltpu.VMEM((2, ROWS, N), BF16),
            pltpu.VMEM((2, ROWS, N), BF16),
            pltpu.VMEM((ROWS, R), F32),
            pltpu.VMEM((2, R, ROWS), BF16),
            pltpu.VMEM((ROWS, N), F32),
            pltpu.VMEM((ROWS, N), F32),
            pltpu.VMEM((ROWS, N), F32),
            pltpu.VMEM((2, PIECE, N // 2), F32),
            pltpu.VMEM((2, PIECE, N // 2), F32),
            pltpu.VMEM((2, PIECE, N), F32),
            pltpu.VMEM((ROWS, N), F32),
            pltpu.VMEM((2, ROWS, N), BF16),
            pltpu.VMEM((3, R, N), F32),
            pltpu.VMEM((2, R, N), F32),
            pltpu.VMEM((R, N), F32),
            pltpu.VMEM((R, 2 * R), F32),
            pltpu.VMEM((R, R), F32),
            pltpu.VMEM((R, R), F32),
            pltpu.VMEM((3, 3, 64, N), F32),
            pltpu.VMEM((3, 64, N), F32),
            pltpu.VMEM((3, 3, 16, N), F32),
            pltpu.VMEM((3, 4, 16, N), F32),
            pltpu.VMEM((4, 2, 64, N // 4), F32),
            pltpu.VMEM((4, 2, 64, N // 4), F32),
            pltpu.VMEM((4, 2, 64, N // 2), F32),
            pltpu.VMEM((4, 64, N // 2), F32),
            pltpu.VMEM((4, 3, 16, N // 2), F32),
            pltpu.VMEM((2, R, N), F32),
            pltpu.VMEM((2, R, R), F32),
            pltpu.VMEM((3, 64, R), F32),
            pltpu.VMEM((64, R), F32),
            pltpu.VMEM((3, 16, R), F32),
            pltpu.SemaphoreType.DMA((17,)),
            pltpu.SemaphoreType.DMA((COPIES,)),
            pltpu.SemaphoreType.DMA((COPIES,)),
        ],
        compiler_params=pltpu.CompilerParams(
            collective_id=0, has_side_effects=True, vmem_limit_bytes=60 * 1024 * 1024
        ),
    )(grads, error, proj_old)
    inputs = (wide, mixer, local, grads, error, cross, summed, moment1, moment2)
    outputs = (
        shape((2, ROWS, N), BF16),
        shape((2, ROWS, N), BF16),
        shape((2, ROWS, R), F32),
        shape((2, R, N), F32),
        shape((2, R, N), F32),
    )
    update, error_new, proj_new, first_new, second_new = pl.pallas_call(
        final_kernel,
        out_shape=outputs,
        in_specs=[anywhere] * 9,
        out_specs=(anywhere,) * 5,
        scratch_shapes=[pltpu.VMEM(one.shape, one.dtype) for one in inputs + outputs]
        + [pltpu.SemaphoreType.DMA((2, 15)), pltpu.SemaphoreType.DMA((18,))],
        compiler_params=pltpu.CompilerParams(vmem_limit_bytes=60 * 1024 * 1024),
    )(*inputs)
    return (update, error_new[None], proj_new, first_new, second_new)


def solution(mesh):
    in_specs = (
        P("dp", None, "fsdp", None),
        P("dp", None, "fsdp", None),
        P(None, "fsdp", None),
        P(),
        P(),
    )
    out_specs = (
        P(None, "fsdp", None),
        P("dp", None, "fsdp", None),
        P(None, "fsdp", None),
        P(),
        P(),
    )
    return jax.shard_map(
        on_device, mesh=mesh, in_specs=in_specs, out_specs=out_specs, check_vma=False
    )
```
